32 devices in a mesh: row: 8 (over z, y), col: 4 (over x, core).
Axes of the slice: x: 2, y: 2, z: 4, core: 2. Of those that a mesh axis runs over, the one named last changes fastest.
Arguments:
- trail_adjoint: float32 [6144, 6144], P('row', 'col'), may hold values from -3 to 3
- panel: float32 [6144, 256], P(('row', 'col')), may hold values from -0.078125 to 0.078125
- panel_adjoint: float32 [6144, 256], P(('row', 'col')), may hold values from -6 to 6
- diag_factor: float32 [256, 256], replicated, as said below
- diag_inverse: float32 [256, 256], replicated, as said below
- diag_adjoint: float32 [256, 256], replicated, may hold values from -6 to 6
Outputs:
- panel_grad: float32 [6144, 256], P(('row', 'col'))
- diag_grad: float32 [256, 256], replicated
The draws below stay inside these ranges and needn't reach their ends.
Inputs may be any that keep to these rules, and one draw needn't show every extreme that they name: diag_factor is lower triangular with a diagonal between 1 and 2, and diag_inverse is its inverse. diag_factor is lower triangular with a diagonal between 1 and 2.
All inputs are finite; a program needn't handle non-finite values.
Results may differ from the reference program's by a relative error of at most 0.000057.
Values sent between devices are 32-bit elements; how exact they have to be, the bound alone decides.
No kernel may reach another device: no remote copies, remote signals or barrier semaphores. Data moves between devices by JAX's collectives and lax.ppermute only.
A program may use at most 128 MiB of HBM per device.

```python
import math
import jax
import jax.numpy as jnp
from jax import lax

B = 256
M = 6144


def triangle_block(key):
    diag_key = jax.random.fold_in(key, 11)
    off_key = jax.random.fold_in(key, 12)
    diagonal = jnp.exp(jax.random.uniform(diag_key, (B,), jnp.float32) * math.log(2.0))
    off_part = jax.random.normal(off_key, (B, B), jnp.float32) * (0.5 / math.sqrt(B))
    return jnp.tril(off_part, -1) + jnp.diag(diagonal)


def draw_diag_factor(key, part):
    return triangle_block(key)


def draw_diag_inverse(key, part):
    factor = triangle_block(key)
    return jax.scipy.linalg.solve_triangular(factor, jnp.eye(B, dtype=jnp.float32), lower=True)


def level_of(rng, shape, pieces, low, top_value):
    factor_of = 1.0
    for dim, blocks in pieces:
        draws = jax.random.uniform(jax.random.fold_in(jax.random.fold_in(rng, 6), dim), (blocks,), jnp.float32, low / len(pieces), top_value / len(pieces))
        factor_of = factor_of * jnp.repeat(jnp.exp(draws), shape[dim] // blocks).reshape((-1,) + (1,) * (len(shape) - 1 - dim))
    return factor_of


def gaussian(key, dims, scale, bound, cuts=(), kind=jnp.bfloat16):
    array = scale * jax.random.normal(key, dims, jnp.float32)
    if cuts:
        array = array * level_of(key, dims, cuts, -0.22, 0.18)
    return jnp.clip(array, -bound, bound).astype(kind)


def setup_inputs(seed: int = 0) -> dict:
    streams_of = jax.random.split(jax.random.key(seed), 7)
    return {
        "trail_adjoint": gaussian(streams_of[0], (M, M), 0.5, 3.0, ((0, 8), (1, 4)), jnp.float32),
        "panel": gaussian(streams_of[1], (M, B), M ** -0.5, 0.078125, ((0, 32),), jnp.float32),
        "panel_adjoint": gaussian(streams_of[2], (M, B), 1.0, 6.0, ((0, 32),), jnp.float32),
        "diag_factor": draw_diag_factor(jax.random.fold_in(streams_of[6], 71), 0),
        "diag_inverse": draw_diag_inverse(jax.random.fold_in(streams_of[6], 71), 0),
        "diag_adjoint": gaussian(streams_of[5], (B, B), 1.0, 6.0, (), jnp.float32),
    }


def lower_half(matrix):
    return jnp.tril(matrix) - 0.5 * jnp.diag(jnp.diag(matrix))

def reference(trail_adjoint, panel, panel_adjoint, diag_factor, diag_inverse, diag_adjoint):
    highest = lax.Precision.HIGHEST
    image = jnp.dot(trail_adjoint.astype(jnp.float32), panel.astype(jnp.float32), precision=highest, preferred_element_type=jnp.float32)
    updated = panel_adjoint - 2.0 * image
    panel_grad = jnp.dot(updated.astype(jnp.float32), diag_inverse.astype(jnp.float32), precision=highest, preferred_element_type=jnp.float32)
    gram = jnp.dot(panel_grad.T.astype(jnp.float32), panel.astype(jnp.float32), precision=highest, preferred_element_type=jnp.float32)
    corner = diag_adjoint - gram
    inner = lower_half(jnp.dot(diag_factor.T.astype(jnp.float32), corner.astype(jnp.float32), precision=highest, preferred_element_type=jnp.float32))
    left_part = jnp.dot(diag_inverse.T.astype(jnp.float32), inner.astype(jnp.float32), precision=highest, preferred_element_type=jnp.float32)
    diag_grad = lower_half(jnp.dot(left_part.astype(jnp.float32), diag_inverse.astype(jnp.float32), precision=highest, preferred_element_type=jnp.float32))
    return (panel_grad, diag_grad)
```

```python
import jax
import jax.numpy as jnp
from jax import lax
from jax.sharding import PartitionSpec as P

HIGHEST = lax.Precision.HIGHEST
HIGH = lax.Precision.HIGH
AXES = ("row", "col")


def dot(a, b, precision=HIGHEST):
    return jnp.dot(a, b, precision=precision, preferred_element_type=jnp.float32)


def dot_t(a, b, precision=HIGHEST):
    return lax.dot_general(
        a, b, (((0,), (0,)), ((), ())), precision=precision, preferred_element_type=jnp.float32
    )


def lower_half(matrix):
    return jnp.tril(matrix) - 0.5 * jnp.diag(jnp.diag(matrix))


def make_on_device(rows, cols):
    group = rows // cols
    devices = rows * cols

    def index(plane, y, c):
        return (plane * group + y) * cols + c

    def plane_flip(mask):
        return [
            (index(p, y, c), index(p ^ mask, y, c))
            for p in range(cols) for y in range(group) for c in range(cols)
        ]

    def col_flip(mask):
        return [(r * cols + c, r * cols + (c ^ mask)) for r in range(rows) for c in range(cols)]

    planes = [[index(p, y, c) for y in range(group) for c in range(cols)] for p in range(cols)]

    def flip_plane(x, mask):
        return lax.ppermute(x, AXES, plane_flip(mask))

    def flip_col(x, mask):
        return lax.ppermute(x, AXES, col_flip(mask))

    def place(pieces, position):
        height = pieces[0].shape[0]
        out = jnp.zeros((len(pieces) * height,) + pieces[0].shape[1:], pieces[0].dtype)
        for d, piece in enumerate(pieces):
            out = lax.dynamic_update_slice_in_dim(out, piece, (position ^ d) * height, 0)
        return out

    def along_planes(panel, plane):
        pieces = [panel] + [None] * (cols - 1)
        if cols == 4:
            pieces[3] = flip_plane(panel, 3)
            pieces[1] = flip_plane(panel, 1)
            pieces[2] = flip_plane(pieces[3], 1)
        else:
            for d in range(1, cols):
                pieces[d] = flip_plane(panel, d)
        return place(pieces, plane)

    def on_device(trail_adjoint, panel, panel_adjoint, diag_factor, diag_inverse, diag_adjoint):
        size = panel.shape[1]
        height = panel.shape[0]
        row_place = lax.axis_index("row")
        col_place = lax.axis_index("col")
        me = row_place * cols + col_place

        by_plane = along_planes(panel, row_place // group)
        row_pieces = [panel]
        mask = cols // 2
        gathered = panel[None]
        order = [0]
        while mask:
            other = flip_col(gathered, mask)
            gathered = jnp.concatenate([gathered, other])
            order = order + [o ^ mask for o in order]
            mask //= 2
        row_pieces = [gathered[order.index(d)] for d in range(cols)]
        row_panel = place(row_pieces, col_place)

        column_panel = lax.all_to_all(
            jnp.concatenate([by_plane] * group), AXES, 0, 0, axis_index_groups=planes, tiled=True
        )
        partial = dot(trail_adjoint, column_panel, HIGH)
        gram_t = dot_t(panel, panel_adjoint) - 2.0 * dot_t(row_panel, partial)

        held = partial.reshape(cols, height, size)
        mask = cols // 2
        while mask:
            bit = (col_place // mask) % 2
            halves = held.reshape(2, held.shape[0] // 2, height, size)
            mine = lax.dynamic_index_in_dim(halves, bit, 0, keepdims=False)
            theirs = lax.dynamic_index_in_dim(halves, 1 - bit, 0, keepdims=False)
            held = mine + flip_col(theirs, mask)
            mask //= 2
        image = held[0]

        share = size // devices
        summed = jnp.sum(
            lax.all_to_all(gram_t, AXES, 0, 0, tiled=True).reshape(devices, share, size), axis=0
        )
        corner_t = lax.dynamic_slice_in_dim(diag_adjoint, me * share, share, 1).T - dot(
            summed, diag_inverse
        )
        inner_t = dot(corner_t, diag_factor)
        at = lax.broadcasted_iota(jnp.int32, inner_t.shape, 0) + me * share
        across = lax.broadcasted_iota(jnp.int32, inner_t.shape, 1)
        inner_t = jnp.where(across > at, inner_t, jnp.where(across == at, 0.5 * inner_t, 0.0))
        left_t = dot(inner_t, diag_inverse)
        left_t = lax.all_to_all(jnp.tile(left_t, (devices, 1)), AXES, 0, 0, tiled=True)
        diag_grad = lower_half(dot_t(left_t, diag_inverse))

        panel_grad = dot(panel_adjoint - 2.0 * image, diag_inverse)
        return panel_grad, diag_grad

    return on_device


def solution(mesh):
    in_specs = (P("row", "col"), P(("row", "col"), None), P(("row", "col"), None), P(), P(), P())
    out_specs = (P(("row", "col"), None), P())
    return jax.shard_map(
        make_on_device(mesh.shape["row"], mesh.shape["col"]),
        mesh=mesh, in_specs=in_specs, out_specs=out_specs, check_vma=False,
    )
```

```python
import functools

import jax
import jax.numpy as jnp
from jax import lax
from jax.experimental import pallas as pl
from jax.experimental.pallas import tpu as pltpu
from jax.sharding import PartitionSpec as P

HIGHEST = lax.Precision.HIGHEST
AXES = ("row", "col")
VMEM = pl.BlockSpec(memory_space=pltpu.VMEM)
SMEM = pl.BlockSpec(memory_space=pltpu.SMEM)
LIMIT = 48 * 1024 * 1024


def dot(a, b, precision=HIGHEST):
    return jnp.dot(a, b, precision=precision, preferred_element_type=jnp.float32)


def dot_t(a, b, precision=HIGHEST):
    return lax.dot_general(
        a, b, (((0,), (0,)), ((), ())), precision=precision, preferred_element_type=jnp.float32
    )


def parts(x):
    high = lax.reduce_precision(x, 8, 7)
    return high.astype(jnp.bfloat16), (x - high).astype(jnp.bfloat16)


def kernel_parts(x):
    high = x.astype(jnp.bfloat16)
    return high, (x - high.astype(jnp.float32)).astype(jnp.bfloat16)


def product_kernel(
    group, cols, height, half, last,
    place, a_high, a_low, pieces, rowt_high, rowt_low, start, before, keep, send, gram_t, wide, split,
):
    step = pl.program_id(0)
    col, plane = place[0], place[1]

    @pl.when(step == 0)
    def _():
        for y in range(group):
            for c in range(cols):
                high, low = kernel_parts(pieces[y * cols + (plane ^ c)])
                at = pl.ds((y * cols + c) * height, height)
                wide[at, :half] = high
                wide[at, half:] = low

    both = dot(a_high[...], wide[...], None) + dot(a_low[...], wide[...], None)
    block = both[:, :half] + both[:, half:]
    target = step ^ col
    near = cols // 2

    @pl.when(target < near)
    def _():
        keep[target] = block

    @pl.when(target >= near)
    def _():
        send[target - near] = block

    at = pl.ds(pl.multiple_of(step * height, height), height)
    high, low = kernel_parts(block)
    split[at, :half] = high
    split[at, half:] = low

    @pl.when(step == cols - 1)
    def _():
        total = dot(rowt_high[...], split[...], None) + dot(rowt_low[...], split[...], None)
        total = total[:, :half] + total[:, half:]
        if last:
            gram_t[:, :half] = before[...]
            gram_t[:, half:] = start[:, half:] - 2.0 * total
        else:
            gram_t[...] = start[:, :half] - 2.0 * total


def half_product(place, a_high, a_low, pieces, rowt_high, rowt_low, start, before, group, cols, last):
    rows, width = a_high.shape
    height, half = pieces.shape[1], pieces.shape[2]
    size = rowt_high.shape[0]
    whole = lambda *shape: pl.BlockSpec(shape, lambda i: (0,) * len(shape))
    near = cols // 2
    gram_width = size if last else half
    return pl.pallas_call(
        functools.partial(product_kernel, group, cols, height, half, last),
        grid=(cols,),
        in_specs=[
            SMEM,
            pl.BlockSpec((height, width), lambda i: (i, 0)),
            pl.BlockSpec((height, width), lambda i: (i, 0)),
            whole(*pieces.shape),
            whole(*rowt_high.shape),
            whole(*rowt_low.shape),
            whole(*start.shape),
            whole(*before.shape),
        ],
        out_specs=[whole(near, height, half), whole(cols - near, height, half), whole(size, gram_width)],
        out_shape=[
            jax.ShapeDtypeStruct((near, height, half), jnp.float32),
            jax.ShapeDtypeStruct((cols - near, height, half), jnp.float32),
            jax.ShapeDtypeStruct((size, gram_width), jnp.float32),
        ],
        scratch_shapes=[
            pltpu.VMEM((width, 2 * half), jnp.bfloat16),
            pltpu.VMEM((rows, 2 * half), jnp.bfloat16),
        ],
        compiler_params=pltpu.CompilerParams(vmem_limit_bytes=LIMIT),
        cost_estimate=pl.CostEstimate(
            flops=8 * rows * width * half, bytes_accessed=4 * rows * width, transcendentals=0
        ),
        name="half_product",
    )(place, a_high, a_low, pieces, rowt_high, rowt_low, start, before)


def middle_kernel(devices, share, place, shares, adjoint_t, factor, inverse, out):
    total = shares[pl.ds(0, share), :]
    for i in range(1, devices):
        total = total + shares[pl.ds(i * share, share), :]
    inner_t = dot(adjoint_t[...] - dot(total, inverse[...]), factor[...])
    at = lax.broadcasted_iota(jnp.int32, inner_t.shape, 0) + place[2] * share
    across = lax.broadcasted_iota(jnp.int32, inner_t.shape, 1)
    inner_t = jnp.where(across > at, inner_t, jnp.where(across == at, 0.5 * inner_t, 0.0))
    left_t = dot(inner_t, inverse[...])
    for i in range(devices):
        out[pl.ds(i * share, share), :] = left_t


def last_kernel(left_t, inverse, out):
    full = dot_t(left_t[...], inverse[...])
    at = lax.broadcasted_iota(jnp.int32, full.shape, 0)
    across = lax.broadcasted_iota(jnp.int32, full.shape, 1)
    out[...] = jnp.where(across < at, full, jnp.where(across == at, 0.5 * full, 0.0))


def panel_kernel(count, adjoint, inverse, *refs):
    sums, out = refs[:-1], refs[-1]
    images = [sums[2 * i][...] + sums[2 * i + 1][...] for i in range(count)]
    image = jnp.concatenate(images, axis=1)
    out[...] = dot(adjoint[...] - 2.0 * image, inverse[...])


def call(kernel, shape, *args, name):
    return pl.pallas_call(
        kernel,
        out_shape=jax.ShapeDtypeStruct(shape, jnp.float32),
        in_specs=[SMEM if x.dtype == jnp.int32 else VMEM for x in args],
        out_specs=VMEM,
        compiler_params=pltpu.CompilerParams(vmem_limit_bytes=LIMIT),
        name=name,
    )(*args)


def make_on_device(rows, cols):
    group = rows // cols
    devices = rows * cols

    def index(plane, y, c):
        return (plane * group + y) * cols + c

    def plane_flip(mask):
        return [
            (index(p, y, c), index(p ^ mask, y, c))
            for p in range(cols) for y in range(group) for c in range(cols)
        ]

    def col_flip(mask):
        return [(r * cols + c, r * cols + (c ^ mask)) for r in range(rows) for c in range(cols)]

    planes = [[index(p, y, p ^ d) for y in range(group) for d in range(cols)] for p in range(cols)]

    def flip_plane(x, mask):
        return lax.ppermute(x, AXES, plane_flip(mask))

    def flip_col(x, mask):
        return lax.ppermute(x, AXES, col_flip(mask))

    def along_planes(panel):
        pieces = [panel] + [None] * (cols - 1)
        if cols == 4:
            pieces[3] = flip_plane(panel, 3)
            pieces[1] = flip_plane(panel, 1)
            pieces[2] = flip_plane(pieces[3], 1)
        else:
            for d in range(1, cols):
                pieces[d] = flip_plane(panel, d)
        return pieces

    def of_row(panel, col_place):
        height = panel.shape[0]
        gathered, order, mask = panel[None], [0], cols // 2
        while mask:
            gathered = jnp.concatenate([gathered, flip_col(gathered, mask)])
            order = order + [o ^ mask for o in order]
            mask //= 2
        out = jnp.zeros((cols * height, panel.shape[1]), panel.dtype)
        for i, d in enumerate(order):
            out = lax.dynamic_update_slice_in_dim(out, gathered[i], (col_place ^ d) * height, 0)
        return out

    def on_device(trail_adjoint, panel, panel_adjoint, diag_factor, diag_inverse, diag_adjoint):
        height, size = panel.shape
        half = size // 2
        row_place = lax.axis_index("row")
        col_place = lax.axis_index("col")
        me = row_place * cols + col_place
        place = jnp.stack([col_place, row_place // group, me]).astype(jnp.int32)

        halves = []
        for h in range(2):
            pieces = jnp.stack(along_planes(panel[:, h * half : (h + 1) * half]) * group)
            halves.append(
                lax.all_to_all(pieces, AXES, 0, 0, axis_index_groups=planes, tiled=True)
            )
        rowt_high, rowt_low = parts(of_row(panel, col_place).T)
        a_high, a_low = parts(trail_adjoint)
        start = dot_t(panel, panel_adjoint)

        sums = []
        gram_t = start
        for h in range(2):
            keep, send, gram_t = half_product(
                place, a_high, a_low, halves[h], rowt_high, rowt_low, start, gram_t,
                group, cols, h == 1,
            )
            mask = cols // 2
            while mask:
                came = flip_col(send, mask)
                mask //= 2
                if mask:
                    keep, send = keep[:mask] + came[:mask], keep[mask:] + came[mask:]
            sums += [keep[0], came[0]]

        share = size // devices
        shares = lax.all_to_all(gram_t, AXES, 0, 0, tiled=True)
        adjoint_t = lax.dynamic_slice_in_dim(diag_adjoint.T, me * share, share, 0)
        if share % 8 == 0:
            left_t = call(
                functools.partial(middle_kernel, devices, share), (size, size),
                place, shares, adjoint_t, diag_factor, diag_inverse, name="middle",
            )
        else:
            total = jnp.sum(shares.reshape(devices, share, size), axis=0)
            inner_t = dot(adjoint_t - dot(total, diag_inverse), diag_factor)
            at = lax.broadcasted_iota(jnp.int32, inner_t.shape, 0) + me * share
            across = lax.broadcasted_iota(jnp.int32, inner_t.shape, 1)
            inner_t = jnp.where(across > at, inner_t, jnp.where(across == at, 0.5 * inner_t, 0.0))
            left_t = jnp.tile(dot(inner_t, diag_inverse), (devices, 1))
        left_t = lax.all_to_all(left_t, AXES, 0, 0, tiled=True)
        diag_grad = call(last_kernel, (size, size), left_t, diag_inverse, name="diag_grad")
        panel_grad = call(
            functools.partial(panel_kernel, 2), panel.shape,
            panel_adjoint, diag_inverse, *sums, name="panel_grad",
        )
        return panel_grad, diag_grad

    return on_device


def solution(mesh):
    in_specs = (P("row", "col"), P(("row", "col"), None), P(("row", "col"), None), P(), P(), P())
    out_specs = (P(("row", "col"), None), P())
    return jax.shard_map(
        make_on_device(mesh.shape["row"], mesh.shape["col"]),
        mesh=mesh, in_specs=in_specs, out_specs=out_specs, check_vma=False,
    )
```

```python
import functools

import jax
import jax.numpy as jnp
from jax import lax
from jax.experimental import pallas as pl
from jax.experimental.pallas import tpu as pltpu
from jax.sharding import PartitionSpec as P

HIGHEST = lax.Precision.HIGHEST
AXES = ("row", "col")
ANY = pl.BlockSpec(memory_space=pl.ANY)
VMEM = pl.BlockSpec(memory_space=pltpu.VMEM)
LIMIT = 16 * 1024 * 1024


def dot(a, b, precision=HIGHEST):
    return jnp.dot(a, b, precision=precision, preferred_element_type=jnp.float32)


def dot_t(a, b, precision=HIGHEST):
    return lax.dot_general(
        a, b, (((0,), (0,)), ((), ())), precision=precision, preferred_element_type=jnp.float32
    )


def parts(x):
    high = x.astype(jnp.bfloat16)
    return high, (x - high.astype(jnp.float32)).astype(jnp.bfloat16)


def dot_parts(x, high, low):
    rows = x.shape[0]
    x = jnp.concatenate(parts(x), axis=0)
    both = dot(x, high, None) + dot(x, low, None)
    return both[:rows] + both[rows:]


def halve_kernel(h, x, out):
    half = out.shape[1]
    out[...] = x[:, h * half : (h + 1) * half]


def prepare_kernel(cols, order, *refs):
    blocks, rest = refs[:cols], refs[cols:]
    adjoint, factor, inverse, corner, rowt_high, rowt_low, start, base, unit, inv = rest
    height = adjoint.shape[0]
    for d in range(cols):
        high, low = parts(blocks[order.index(d)][...].T)
        rowt_high[:, d * height : (d + 1) * height] = high
        rowt_low[:, d * height : (d + 1) * height] = low
    start[...] = dot_t(blocks[0][...], adjoint[...])
    base[...] = dot_t(corner[...], factor[...])
    high, low = parts(dot(inverse[...], factor[...]))
    unit[0], unit[1] = high, low
    high, low = parts(inverse[...])
    inv[0], inv[1] = high, low


def assemble_kernel(group, cols, *refs):
    pieces, out = refs[:-1], refs[-1]
    for y in range(group):
        for d in range(cols):
            out[y * cols + d] = pieces[d][...]


def trail_kernel(trail, out):
    out[0], out[1] = parts(trail[...])


def choose_kernel(zero, one, two, three, own, other):
    side = lax.axis_index("col") // 2
    mine = side == lax.axis_index("row") // 4
    for ref, take in ((own, mine), (other, jnp.logical_not(mine))):

        @pl.when(take)
        def _():
            ref[0] = zero[...]
            ref[1] = one[...]

        @pl.when(jnp.logical_not(take))
        def _():
            ref[0] = two[...]
            ref[1] = three[...]


def fill_pieces(group, cols, pieces, wide):
    height, half = pieces.shape[1], pieces.shape[2]
    plane = lax.axis_index("row") // group
    for y in range(group):
        for c in range(cols):
            high, low = parts(pieces[y * cols + (plane ^ c)])
            at = pl.ds((y * cols + c) * height, height)
            wide[at, :half] = high
            wide[at, half:] = low


def which_plane():
    return (lax.axis_index("row") // 2 + lax.axis_index("col")) % 2


def pick_kernel(*refs):
    pairs, out = refs[:-1], refs[-1]
    theirs = 1 - which_plane()
    for i, pair in enumerate(pairs):
        out[i] = pair[theirs]


def fill_pairs(pairs, came, wide):
    height, half = pairs[0].shape[1], pairs[0].shape[2]
    which = which_plane()
    place = lax.axis_index("row") % 2 * 4 + lax.axis_index("col")
    for i in range(2 * len(pairs)):
        k, y, x = i // 4, i // 2 % 2, i % 2
        source = place ^ (y * 4 + x * 2 + k)
        high, low = parts(came[i % 4] if k else pairs[i][which])
        at = pl.ds(pl.multiple_of(source * height, height), height)
        wide[at, :half] = high
        wide[at, half:] = low


def product_kernel(group, cols, count, last, *refs):
    pieces, refs = refs[:count], refs[count:]
    if last:
        rowt_high, rowt_low, start, before, trail, keep, send, gram_t, wide, split = refs
    else:
        rowt_high, rowt_low, start, trail, keep, send, gram_t, _, wide, split = refs
    height, half = pieces[0].shape[1], pieces[0].shape[2]
    col = lax.axis_index("col")
    if count == 1:
        fill_pieces(group, cols, pieces[0], wide)
    else:
        fill_pairs(pieces[:-1], pieces[-1], wide)
    for target in range(cols):
        at = pl.ds(target * height, height)
        both = dot(trail[0, at, :], wide[...], None) + dot(trail[1, at, :], wide[...], None)
        block = both[:, :half] + both[:, half:]
        d = target ^ col
        high, low = parts(block)
        at = pl.ds(pl.multiple_of(d * height, height), height)
        split[at, :half] = high
        split[at, half:] = low

        @pl.when(d % 2 == 0)
        def _():
            keep[d // 2] = block

        @pl.when(d % 2 == 1)
        def _():
            send[d // 2] = block

    total = dot(rowt_high[...], split[...], None) + dot(rowt_low[...], split[...], None)
    total = total[:, :half] + total[:, half:]
    if last:
        gram_t[:, :half] = before[...]
        gram_t[:, half:] = start[:, half:] - 2.0 * total
    else:
        gram_t[...] = start[:, :half] - 2.0 * total


def middle_kernel(devices, cols, share, shares, base, unit, inv, out):
    total = shares[pl.ds(0, share), :]
    for i in range(1, devices):
        total = total + shares[pl.ds(i * share, share), :]
    me = lax.axis_index("row") * cols + lax.axis_index("col")
    first = pl.multiple_of(me * share, share)
    inner_t = base[pl.ds(first, share), :] - dot_parts(total, unit[0], unit[1])
    at = lax.broadcasted_iota(jnp.int32, inner_t.shape, 0) + first
    across = lax.broadcasted_iota(jnp.int32, inner_t.shape, 1)
    inner_t = jnp.where(across > at, inner_t, jnp.where(across == at, 0.5 * inner_t, 0.0))
    left_t = dot_parts(inner_t, inv[0], inv[1])
    for i in range(devices):
        out[pl.ds(i * share, share), :] = left_t


def last_kernel(left_t, inv, out):
    full = dot_parts(left_t[...].T, inv[0], inv[1])
    at = lax.broadcasted_iota(jnp.int32, full.shape, 0)
    across = lax.broadcasted_iota(jnp.int32, full.shape, 1)
    out[...] = jnp.where(across < at, full, jnp.where(across == at, 0.5 * full, 0.0))


def add_kernel(count, *refs):
    half, blocks = refs[0].shape[2], refs[0].shape[0]
    mine, theirs = refs[-2:]
    for h in range(count):
        keep, came = refs[2 * h], refs[2 * h + 1]
        at = slice(h * half, (h + 1) * half)
        for i in range(blocks // 2):
            mine[i, :, at] = keep[2 * i] + came[2 * i]
            theirs[i, :, at] = keep[2 * i + 1] + came[2 * i + 1]


def panel_kernel(adjoint, inv, mine, came, out, inv_on):
    inv_on[...] = inv[...]
    out[...] = dot_parts(adjoint[...] - 2.0 * (mine[0] + came[0]), inv[0], inv[1])


def whole(shape):
    return pl.BlockSpec(shape, lambda i: (0,) * len(shape))


def call(kernel, shapes, *args, name, after=(), cost=1000):
    out = [
        s if isinstance(s, jax.ShapeDtypeStruct) else jax.ShapeDtypeStruct(s, jnp.float32)
        for s in shapes
    ]

    def body(*refs):
        kernel(*refs[: len(args)], *refs[len(args) + len(after) :])

    return pl.pallas_call(
        body,
        grid=(1,),
        out_shape=out,
        in_specs=[whole(x.shape) for x in args] + [ANY] * len(after),
        out_specs=[whole(x.shape) for x in out],
        compiler_params=pltpu.CompilerParams(vmem_limit_bytes=LIMIT),
        cost_estimate=pl.CostEstimate(flops=1000, bytes_accessed=cost, transcendentals=0),
        name=name,
    )(*args, *after)


def split_trail(trail):
    rows, width = trail.shape
    blocks = 4
    return pl.pallas_call(
        trail_kernel,
        grid=(blocks,),
        in_specs=[pl.BlockSpec((rows // blocks, width), lambda i: (i, 0))],
        out_specs=pl.BlockSpec((2, rows // blocks, width), lambda i: (0, i, 0)),
        out_shape=jax.ShapeDtypeStruct((2, rows, width), jnp.bfloat16),
        compiler_params=pltpu.CompilerParams(vmem_limit_bytes=2 * LIMIT),
        cost_estimate=pl.CostEstimate(flops=1000, bytes_accessed=8 * rows * width, transcendentals=0),
        name="split_trail",
    )(trail)


def half_product(trail, pieces, rowt, start, before, group, cols, after=()):
    _, rows, width = trail.shape
    height, half = pieces[0].shape[1], pieces[0].shape[2]
    size = rowt[0].shape[0]
    near = cols // 2
    last = before is not None
    out = [
        jax.ShapeDtypeStruct((near, height, half), jnp.float32),
        jax.ShapeDtypeStruct((cols - near, height, half), jnp.float32),
        jax.ShapeDtypeStruct((size, size if last else half), jnp.float32),
    ]
    args = list(pieces) + list(rowt) + [start] + ([before] if last else [])
    count = len(args) + 1
    kernel = functools.partial(product_kernel, group, cols, len(pieces), last)

    def body(*refs):
        kernel(*refs[:count], *refs[count + len(after) :])

    return pl.pallas_call(
        body,
        grid=(1,),
        in_specs=[VMEM] * (len(args) + 1) + [ANY] * len(after),
        out_specs=[whole(x.shape) for x in out] + ([] if last else [VMEM]),
        out_shape=out + ([] if last else [jax.ShapeDtypeStruct(trail.shape, trail.dtype)]),
        scratch_shapes=[
            pltpu.VMEM((width, 2 * half), jnp.bfloat16),
            pltpu.VMEM((rows, 2 * half), jnp.bfloat16),
        ],
        input_output_aliases={} if last else {count - 1: 3},
        compiler_params=pltpu.CompilerParams(vmem_limit_bytes=LIMIT),
        cost_estimate=pl.CostEstimate(flops=1000, bytes_accessed=8 * rows * width, transcendentals=0),
        name="half_product",
    )(*args, trail, *after)


def make_on_device(rows, cols):
    group = rows // cols
    devices = rows * cols

    def index(plane, y, c):
        return (plane * group + y) * cols + c

    def plane_flip(mask):
        return [
            (index(p, y, c), index(p ^ mask, y, c))
            for p in range(cols) for y in range(group) for c in range(cols)
        ]

    def col_flip(mask):
        return [(r * cols + c, r * cols + (c ^ mask)) for r in range(rows) for c in range(cols)]

    planes = [[index(p, y, p ^ d) for y in range(group) for d in range(cols)] for p in range(cols)]

    def flip_plane(x, mask):
        return lax.ppermute(x, AXES, plane_flip(mask))

    def flip_col(x, mask):
        return lax.ppermute(x, AXES, col_flip(mask))

    def flip_y(x, mask):
        pairs = [
            (r * cols + c, (r ^ 1) * cols + (c ^ mask)) for r in range(rows) for c in range(cols)
        ]
        return lax.ppermute(x, AXES, pairs)

    def on_device(trail_adjoint, panel, panel_adjoint, diag_factor, diag_inverse, diag_adjoint):
        height, size = panel.shape
        half = size // 2
        row_place = lax.axis_index("row")
        col_place = lax.axis_index("col")
        me = row_place * cols + col_place

        far = []
        for h in range(2):
            (mine,) = call(
                functools.partial(halve_kernel, h), [(height, half)], panel,
                name="halve", after=(far[0][1],) if h else (),
            )
            pieces = {0: mine}
            for d in range(3, cols, 2):
                pieces[d] = flip_plane(mine, d)
            pieces[1] = flip_plane(mine, 1)
            for d in range(2, cols, 2):
                pieces[d] = flip_plane(pieces[d + 1], 1)
            far.append([pieces[d] for d in range(cols)])

        blocks, order, mask = [panel], [0], cols // 2
        while mask:
            blocks = blocks + [flip_col(x, mask) for x in blocks]
            order = order + [o ^ mask for o in order]
            mask //= 2
        trail = split_trail(trail_adjoint)
        halves = []
        for h in range(2):
            after = () if h else (blocks[1],)
            if cols == 4 and group == 2:
                own, other = call(
                    choose_kernel, [(2, height, half)] * 2, *far[h], name="choose", after=after
                )
                chosen = own
                halves.append([own, flip_col(other, 2), flip_y(own, 0), flip_y(other, 2)])
            else:
                (chosen,) = call(
                    functools.partial(assemble_kernel, group, cols),
                    [(group * cols, height, half)], *far[h], name="assemble", after=after,
                )
                halves.append([
                    lax.all_to_all(chosen, AXES, 0, 0, axis_index_groups=planes, tiled=True)
                ])

        bf16 = lambda *shape: jax.ShapeDtypeStruct(shape, jnp.bfloat16)
        rowt_high, rowt_low, start, base, unit, inv = call(
            functools.partial(prepare_kernel, cols, order),
            [bf16(size, cols * height)] * 2 + [(size, size)] * 2 + [bf16(2, size, size)] * 2,
            *blocks, panel_adjoint, diag_factor, diag_inverse, diag_adjoint,
            name="prepare", after=(chosen,), cost=1 << 22,
        )

        if len(halves[0]) > 1:
            (theirs,) = call(
                pick_kernel, [(4, height, half)], *halves[0], name="pick", after=(trail, start)
            )
            halves[0].append(flip_col(theirs, 1))
        keep, send, gram_t, trail = half_product(
            trail, halves[0], (rowt_high, rowt_low), start, None, group, cols
        )
        sums = [keep, flip_col(send, 1)]
        if len(halves[1]) > 1:
            (theirs,) = call(
                pick_kernel, [(4, height, half)], *halves[1], name="pick", after=(gram_t,)
            )
            halves[1].append(flip_col(theirs, 1))
        keep, send, gram_t = half_product(
            trail, halves[1], (rowt_high, rowt_low), start, gram_t, group, cols
        )
        sums += [keep, flip_col(send, 1)]

        mine, theirs = call(
            functools.partial(add_kernel, 2), [(cols // 4, height, size)] * 2, *sums, name="add"
        )
        mask = 2
        while True:
            came = flip_col(theirs, mask)
            mask *= 2
            if mask >= cols:
                break
            mine, theirs = mine[::2] + came[::2], mine[1::2] + came[1::2]
        share = size // devices
        shares = lax.all_to_all(gram_t, AXES, 0, 0, tiled=True)
        if share % 8 == 0:
            (left_t,) = call(
                functools.partial(middle_kernel, devices, cols, share), [(size, size)],
                shares, base, unit, inv, name="middle", after=(came,),
            )
        else:
            total = jnp.sum(shares.reshape(devices, share, size), axis=0)
            inner_t = dot(
                lax.dynamic_slice_in_dim(diag_adjoint.T, me * share, share, 0)
                - dot(total, diag_inverse),
                diag_factor,
            )
            at = lax.broadcasted_iota(jnp.int32, inner_t.shape, 0) + me * share
            across = lax.broadcasted_iota(jnp.int32, inner_t.shape, 1)
            inner_t = jnp.where(across > at, inner_t, jnp.where(across == at, 0.5 * inner_t, 0.0))
            left_t = jnp.tile(dot(inner_t, diag_inverse), (devices, 1))
        gathered = lax.all_to_all(left_t, AXES, 0, 0, tiled=True)

        panel_grad, inv = call(
            panel_kernel, [panel.shape, bf16(*inv.shape)], panel_adjoint, inv, mine, came,
            name="panel_grad",
        )
        (diag_grad,) = call(last_kernel, [(size, size)], gathered, inv, name="diag_grad")
        return panel_grad, diag_grad

    return on_device


def solution(mesh):
    in_specs = (P("row", "col"), P(("row", "col"), None), P(("row", "col"), None), P(), P(), P())
    out_specs = (P(("row", "col"), None), P())
    return jax.shard_map(
        make_on_device(mesh.shape["row"], mesh.shape["col"]),
        mesh=mesh, in_specs=in_specs, out_specs=out_specs, check_vma=False,
    )
```

```python
import functools

import jax
import jax.numpy as jnp
from jax import lax
from jax.experimental import pallas as pl
from jax.experimental.pallas import tpu as pltpu
from jax.sharding import PartitionSpec as P

HIGHEST = lax.Precision.HIGHEST
AXES = ("row", "col")
ANY = pl.BlockSpec(memory_space=pl.ANY)
VMEM = pl.BlockSpec(memory_space=pltpu.VMEM)
LIMIT = 16 * 1024 * 1024


def dot(a, b, precision=HIGHEST):
    return jnp.dot(a, b, precision=precision, preferred_element_type=jnp.float32)


def dot_t(a, b, precision=HIGHEST):
    return lax.dot_general(
        a, b, (((0,), (0,)), ((), ())), precision=precision, preferred_element_type=jnp.float32
    )


def parts(x):
    high = x.astype(jnp.bfloat16)
    return high, (x - high.astype(jnp.float32)).astype(jnp.bfloat16)


def dot_parts(x, high, low):
    rows = x.shape[0]
    x = jnp.concatenate(parts(x), axis=0)
    both = dot(x, high, None) + dot(x, low, None)
    return both[:rows] + both[rows:]


def dot_three(a_high, a_low, b_high, b_low):
    return dot(a_high, b_high, None) + dot(a_high, b_low, None) + dot(a_low, b_high, None)


def needs_first():
    return (lax.axis_index("row") // 2 + lax.axis_index("col")) % 2 == 1


def choose_kernel(near, far, own, other):
    mine = lax.axis_index("col") // 2 == lax.axis_index("row") // 4

    @pl.when(mine)
    def _():
        own[...] = near[...]
        other[...] = far[...]

    @pl.when(jnp.logical_not(mine))
    def _():
        own[...] = far[...]
        other[...] = near[...]


def pick_kernel(count, *refs):
    first, second, out = refs[:count], refs[count : 2 * count], refs[-1]

    @pl.when(needs_first())
    def _():
        for i, ref in enumerate(second):
            out[i] = ref[...]

    @pl.when(jnp.logical_not(needs_first()))
    def _():
        for i, ref in enumerate(first):
            out[i] = ref[...]


def prepare_kernel(
    cols, order, blocks, *refs,
):
    rows_of, rest = refs[:cols], refs[cols:]
    (
        adjoint, factor, inverse, corner, trail,
        rowt, start, base, unit, inv, trail_parts, landing, sems,
    ) = rest
    rows = trail.shape[0] // blocks
    copies = []
    for i in range(blocks):
        at = pl.ds(i * rows, rows)
        copies.append(pltpu.make_async_copy(trail.at[at], landing.at[at], sems.at[i]))
        copies[-1].start()
    height = adjoint.shape[0]
    for d in range(cols):
        high, low = parts(rows_of[order.index(d)][...].T)
        rowt[0, :, d * height : (d + 1) * height] = high
        rowt[1, :, d * height : (d + 1) * height] = low
    start[...] = dot_t(rows_of[0][...], adjoint[...])
    base[...] = dot_t(corner[...], factor[...])
    high, low = parts(dot(inverse[...], factor[...]))
    unit[0], unit[1] = high, low
    high, low = parts(inverse[...])
    inv[0], inv[1] = high, low
    for i in range(blocks):
        copies[i].wait()
        at = pl.ds(i * rows, rows)
        trail_parts[0, at, :], trail_parts[1, at, :] = parts(landing[at, :])


def fill_all(group, cols, pieces, wide):
    height = pieces.shape[1]
    plane = lax.axis_index("row") // group
    for y in range(group):
        for c in range(cols):
            at = pl.ds((y * cols + c) * height, height)
            wide[0, at, :], wide[1, at, :] = parts(pieces[y * cols + (plane ^ c)])


def fill_sets(first, second, came, wide):
    height = came.shape[1]
    place = lax.axis_index("row") % 2 * 4 + lax.axis_index("col")

    def put(source, value):
        at = pl.ds(pl.multiple_of(source * height, height), height)
        wide[0, at, :], wide[1, at, :] = parts(value)

    @pl.when(needs_first())
    def _():
        for i, ref in enumerate(first):
            put(place ^ (2 * i), ref[...])

    @pl.when(jnp.logical_not(needs_first()))
    def _():
        for i, ref in enumerate(second):
            put(place ^ (2 * i), ref[...])

    for i in range(came.shape[0]):
        put(place ^ (2 * i) ^ 1, came[i])


def product_kernel(group, cols, count, *refs):
    pieces, (rowt, start, trail, keep, send, gram_t, wide, split) = refs[:count], refs[count:]
    if count == 1:
        fill_all(group, cols, pieces[0], wide)
    else:
        fill_sets(pieces[0:4], pieces[4:8], pieces[8], wide)
    height = split.shape[1] // cols
    col = lax.axis_index("col")
    for target in range(cols):
        at = pl.ds(target * height, height)
        block = dot_three(trail[0, at, :], trail[1, at, :], wide[0], wide[1])
        d = target ^ col
        at = pl.ds(pl.multiple_of(d * height, height), height)
        split[0, at, :], split[1, at, :] = parts(block)

        @pl.when(d % 2 == 0)
        def _():
            keep[d // 2] = block

        @pl.when(d % 2 == 1)
        def _():
            send[d // 2] = block

    gram_t[...] = start[...] - 2.0 * dot_three(rowt[0], rowt[1], split[0], split[1])


def middle_kernel(devices, cols, share, shares, base, unit, inv, out):
    total = shares[pl.ds(0, share), :]
    for i in range(1, devices):
        total = total + shares[pl.ds(i * share, share), :]
    me = lax.axis_index("row") * cols + lax.axis_index("col")
    first = pl.multiple_of(me * share, share)
    inner_t = base[pl.ds(first, share), :] - dot_parts(total, unit[0], unit[1])
    at = lax.broadcasted_iota(jnp.int32, inner_t.shape, 0) + first
    across = lax.broadcasted_iota(jnp.int32, inner_t.shape, 1)
    inner_t = jnp.where(across > at, inner_t, jnp.where(across == at, 0.5 * inner_t, 0.0))
    left_t = dot_parts(inner_t, inv[0], inv[1])
    for i in range(devices):
        out[pl.ds(i * share, share), :] = left_t


def last_kernel(left_t, inv, out):
    full = dot_parts(left_t[...].T, inv[0], inv[1])
    at = lax.broadcasted_iota(jnp.int32, full.shape, 0)
    across = lax.broadcasted_iota(jnp.int32, full.shape, 1)
    out[...] = jnp.where(across < at, full, jnp.where(across == at, 0.5 * full, 0.0))


def add_kernel(keep, came, mine, theirs):
    for i in range(keep.shape[0] // 2):
        mine[i] = keep[2 * i] + came[2 * i]
        theirs[i] = keep[2 * i + 1] + came[2 * i + 1]


def panel_kernel(adjoint, inv, mine, came, out, inv_on):
    inv_on[...] = inv[...]
    out[...] = dot_parts(adjoint[...] - 2.0 * (mine[0] + came[0]), inv[0], inv[1])


def whole(shape):
    return pl.BlockSpec(shape, lambda i: (0,) * len(shape))


def f32(*shape):
    return jax.ShapeDtypeStruct(shape, jnp.float32)


def bf16(*shape):
    return jax.ShapeDtypeStruct(shape, jnp.bfloat16)


def call(
    kernel, out, *args, name, after=(), in_specs=None, out_specs=None, scratch=(), aliases=None
):
    def body(*refs):
        kernel(*refs[: len(args)], *refs[len(args) + len(after) :])

    return pl.pallas_call(
        body,
        grid=(1,),
        out_shape=out,
        in_specs=(in_specs or [whole(x.shape) for x in args]) + [ANY] * len(after),
        out_specs=out_specs or [whole(x.shape) for x in out],
        scratch_shapes=list(scratch),
        input_output_aliases=aliases or {},
        compiler_params=pltpu.CompilerParams(vmem_limit_bytes=LIMIT),
        cost_estimate=pl.CostEstimate(flops=1000, bytes_accessed=1000, transcendentals=0),
        name=name,
    )(*args, *after)


def make_on_device(rows, cols):
    group = rows // cols
    devices = rows * cols
    paired = cols == 4 and group == 2

    def index(plane, y, c):
        return (plane * group + y) * cols + c

    planes = [[index(p, y, p ^ d) for y in range(group) for d in range(cols)] for p in range(cols)]

    def flip(x, plane=0, y=0, col=0):
        pairs = [
            (index(p, v, c), index(p ^ plane, v ^ y, c ^ col))
            for p in range(cols) for v in range(group) for c in range(cols)
        ]
        return lax.ppermute(x, AXES, pairs)

    def on_device(trail_adjoint, panel, panel_adjoint, diag_factor, diag_inverse, diag_adjoint):
        height, size = panel.shape
        width = trail_adjoint.shape[1]
        me = lax.axis_index("row") * cols + lax.axis_index("col")

        pieces = {0: panel}
        for d in range(3, cols, 2):
            pieces[d] = flip(panel, plane=d)
        pieces[1] = flip(panel, plane=1)
        for d in range(2, cols, 2):
            pieces[d] = flip(pieces[d + 1], plane=1)

        row_blocks, order, mask = [panel], [0], cols // 2
        while mask:
            row_blocks = row_blocks + [flip(x, col=mask) for x in row_blocks]
            order = order + [o ^ mask for o in order]
            mask //= 2

        if paired:
            sets = []
            for near, far in ((1, 3), (0, 2)):
                own, other = call(
                    choose_kernel, [f32(height, size)] * 2, pieces[near], pieces[far],
                    name="choose", after=(row_blocks[1],) if near else (),
                )
                sets.append([own, flip(other, col=2), flip(own, y=1), flip(other, y=1, col=2)])
            chosen = own
        else:
            chosen = jnp.stack([pieces[d] for d in range(cols)] * group)

        blocks = 4
        rowt, start, base, unit, inv, trail = call(
            functools.partial(prepare_kernel, cols, order, blocks),
            [bf16(2, size, cols * height), f32(size, size), f32(size, size)]
            + [bf16(2, size, size)] * 2 + [bf16(2, *trail_adjoint.shape)],
            *row_blocks, panel_adjoint, diag_factor, diag_inverse, diag_adjoint, trail_adjoint,
            name="prepare", after=(chosen,),
            in_specs=[whole(panel.shape)] * (cols + 1) + [whole((size, size))] * 3 + [ANY],
            out_specs=[VMEM] * 6,
            scratch=[
                pltpu.VMEM(trail_adjoint.shape, jnp.float32), pltpu.SemaphoreType.DMA((blocks,)),
            ],
        )

        if paired:
            args = sets[0] + sets[1]
            theirs = call(
                functools.partial(pick_kernel, 4), [f32(4, height, size)], *args,
                name="pick", after=(trail,),
            )[0]
            args = args + [flip(theirs, col=1)]
        else:
            args = [lax.all_to_all(chosen, AXES, 0, 0, axis_index_groups=planes, tiled=True)]
        keep, send, gram_t = call(
            functools.partial(product_kernel, group, cols, len(args)),
            [f32(cols // 2, height, size)] * 2 + [f32(size, size)],
            *args, rowt, start, trail, name="product", in_specs=[VMEM] * (len(args) + 3),
            scratch=[
                pltpu.VMEM((2, width, size), jnp.bfloat16),
                pltpu.VMEM((2, cols * height, size), jnp.bfloat16),
            ],
        )

        mine, theirs = call(
            add_kernel, [f32(cols // 4, height, size)] * 2, keep, flip(send, col=1), name="add"
        )
        mask = 2
        while True:
            came = flip(theirs, col=mask)
            mask *= 2
            if mask >= cols:
                break
            mine, theirs = mine[::2] + came[::2], mine[1::2] + came[1::2]

        share = size // devices
        shares = lax.all_to_all(gram_t, AXES, 0, 0, tiled=True)
        if share % 8 == 0:
            (left_t,) = call(
                functools.partial(middle_kernel, devices, cols, share), [f32(size, size)],
                shares, base, unit, inv, name="middle", after=(theirs,),
            )
        else:
            total = jnp.sum(shares.reshape(devices, share, size), axis=0)
            inner_t = dot(
                lax.dynamic_slice_in_dim(diag_adjoint.T, me * share, share, 0)
                - dot(total, diag_inverse),
                diag_factor,
            )
            at = lax.broadcasted_iota(jnp.int32, inner_t.shape, 0) + me * share
            across = lax.broadcasted_iota(jnp.int32, inner_t.shape, 1)
            inner_t = jnp.where(across > at, inner_t, jnp.where(across == at, 0.5 * inner_t, 0.0))
            left_t = jnp.tile(dot(inner_t, diag_inverse), (devices, 1))
        gathered = lax.all_to_all(left_t, AXES, 0, 0, tiled=True)

        panel_grad, inv = call(
            panel_kernel, [f32(*panel.shape), bf16(*inv.shape)], panel_adjoint, inv, mine, came,
            name="panel_grad",
        )
        (diag_grad,) = call(last_kernel, [f32(size, size)], gathered, inv, name="diag_grad")
        return panel_grad, diag_grad

    return on_device


def solution(mesh):
    in_specs = (P("row", "col"), P(("row", "col"), None), P(("row", "col"), None), P(), P(), P())
    out_specs = (P(("row", "col"), None), P())
    return jax.shard_map(
        make_on_device(mesh.shape["row"], mesh.shape["col"]),
        mesh=mesh, in_specs=in_specs, out_specs=out_specs, check_vma=False,
    )
```

```python
import functools

import jax
import jax.numpy as jnp
from jax import lax
from jax.experimental import pallas as pl
from jax.experimental.pallas import tpu as pltpu
from jax.sharding import PartitionSpec as P

HIGHEST = lax.Precision.HIGHEST
AXES = ("row", "col")
ANY = pl.BlockSpec(memory_space=pl.ANY)
VMEM = pl.BlockSpec(memory_space=pltpu.VMEM)
LIMIT = 16 * 1024 * 1024


def dot(a, b, precision=HIGHEST):
    return jnp.dot(a, b, precision=precision, preferred_element_type=jnp.float32)


def dot_t(a, b, precision=HIGHEST):
    return lax.dot_general(
        a, b, (((0,), (0,)), ((), ())), precision=precision, preferred_element_type=jnp.float32
    )


def parts(x):
    high = x.astype(jnp.bfloat16)
    return high, (x - high.astype(jnp.float32)).astype(jnp.bfloat16)


def dot_parts(x, high, low):
    rows = x.shape[0]
    x = jnp.concatenate(parts(x), axis=0)
    both = dot(x, high, None) + dot(x, low, None)
    return both[:rows] + both[rows:]


def dot_three(a_high, a_low, b_high, b_low):
    return dot(a_high, b_high, None) + dot(a_high, b_low, None) + dot(a_low, b_high, None)


def needs_first():
    return (lax.axis_index("row") // 2 + lax.axis_index("col")) % 2 == 1


def choose_kernel(near, far, own, other):
    mine = lax.axis_index("col") // 2 == lax.axis_index("row") // 4

    @pl.when(mine)
    def _():
        own[...] = near[...]
        other[...] = far[...]

    @pl.when(jnp.logical_not(mine))
    def _():
        own[...] = far[...]
        other[...] = near[...]


def pick_kernel(count, *refs):
    first, second, out = refs[:count], refs[count : 2 * count], refs[-1]

    @pl.when(needs_first())
    def _():
        for i, ref in enumerate(second):
            out[i] = ref[...]

    @pl.when(jnp.logical_not(needs_first()))
    def _():
        for i, ref in enumerate(first):
            out[i] = ref[...]


def prepare_kernel(blocks, places, *refs):
    rows_of, refs = refs[: len(places)], refs[len(places) :]
    panel, adjoint, factor, inverse, corner, trail = refs[:6]
    rowt, start, base, unit, inv, trail_parts = refs[6:12]
    landing, here, sems = refs[12], refs[13:-1], refs[-1]
    rows = trail.shape[0] // blocks
    small = [
        pltpu.make_async_copy(ref, to, sems.at[blocks + i])
        for i, (ref, to) in enumerate(zip((panel, adjoint, factor, inverse, corner), here))
    ]
    large = []
    for i in range(blocks):
        at = pl.ds(i * rows, rows)
        large.append(pltpu.make_async_copy(trail.at[at], landing.at[at], sems.at[i]))
    for copy in small + large:
        copy.start()
    for copy in small:
        copy.wait()
    panel, adjoint, factor, inverse, corner = here
    height = adjoint.shape[0]
    for d, block in enumerate([panel] + [rows_of[i] for i in places]):
        high, low = parts(block[...].T)
        rowt[0, :, d * height : (d + 1) * height] = high
        rowt[1, :, d * height : (d + 1) * height] = low
    start[...] = dot_t(panel[...], adjoint[...])
    base[...] = dot_t(corner[...], factor[...])
    unit[0], unit[1] = parts(dot(inverse[...], factor[...]))
    inv[0], inv[1] = parts(inverse[...])
    for i in range(blocks):
        large[i].wait()
        at = pl.ds(i * rows, rows)
        trail_parts[0, at, :], trail_parts[1, at, :] = parts(landing[at, :])


def fill_all(group, cols, pieces, wide):
    height = pieces.shape[1]
    plane = lax.axis_index("row") // group
    for y in range(group):
        for c in range(cols):
            at = pl.ds((y * cols + c) * height, height)
            wide[0, at, :], wide[1, at, :] = parts(pieces[y * cols + (plane ^ c)])


def fill_sets(first, second, came, wide):
    height = came.shape[1]
    place = lax.axis_index("row") % 2 * 4 + lax.axis_index("col")

    def put(source, value):
        at = pl.ds(pl.multiple_of(source * height, height), height)
        wide[0, at, :], wide[1, at, :] = parts(value)

    @pl.when(needs_first())
    def _():
        for i, ref in enumerate(first):
            put(place ^ (2 * i), ref[...])

    @pl.when(jnp.logical_not(needs_first()))
    def _():
        for i, ref in enumerate(second):
            put(place ^ (2 * i), ref[...])

    for i in range(came.shape[0]):
        put(place ^ (2 * i) ^ 1, came[i])


def product_kernel(group, cols, count, *refs):
    pieces, (rowt, start, trail, keep, send, gram_t, wide, split, image) = refs[:count], refs[count:]
    if count == 1:
        fill_all(group, cols, pieces[0], wide)
    else:
        fill_sets(pieces[0:4], pieces[4:8], pieces[8], wide)
    height = image.shape[0] // cols
    for i in range(cols):
        at = pl.ds(i * height, height)
        image[at, :] = dot_three(trail[0, at, :], trail[1, at, :], wide[0], wide[1])
    col = lax.axis_index("col")
    for d in range(cols):
        block = image[pl.ds(pl.multiple_of((d ^ col) * height, height), height), :]
        at = pl.ds(d * height, height)
        split[0, at, :], split[1, at, :] = parts(block)
        (send if d % 2 else keep)[d // 2] = block
    gram_t[...] = start[...] - 2.0 * dot_three(rowt[0], rowt[1], split[0], split[1])


def middle_kernel(devices, cols, share, shares, base, unit, inv, out):
    total = shares[pl.ds(0, share), :]
    for i in range(1, devices):
        total = total + shares[pl.ds(i * share, share), :]
    me = lax.axis_index("row") * cols + lax.axis_index("col")
    first = pl.multiple_of(me * share, share)
    inner_t = base[pl.ds(first, share), :] - dot_parts(total, unit[0], unit[1])
    at = lax.broadcasted_iota(jnp.int32, inner_t.shape, 0) + first
    across = lax.broadcasted_iota(jnp.int32, inner_t.shape, 1)
    inner_t = jnp.where(across > at, inner_t, jnp.where(across == at, 0.5 * inner_t, 0.0))
    left_t = dot_parts(inner_t, inv[0], inv[1])
    for i in range(devices):
        out[pl.ds(i * share, share), :] = left_t


def last_kernel(left_t, inv, out):
    full = dot_parts(left_t[...].T, inv[0], inv[1])
    at = lax.broadcasted_iota(jnp.int32, full.shape, 0)
    across = lax.broadcasted_iota(jnp.int32, full.shape, 1)
    out[...] = jnp.where(across < at, full, jnp.where(across == at, 0.5 * full, 0.0))


def add_kernel(keep, came, adjoint, inv, mine, theirs):
    for i in range(keep.shape[0] // 2):
        own = -2.0 * (keep[2 * i] + came[2 * i])
        mine[i] = dot_parts(own if i else adjoint[...] + own, inv[0], inv[1])
        theirs[i] = dot_parts(-2.0 * (keep[2 * i + 1] + came[2 * i + 1]), inv[0], inv[1])


def panel_kernel(mine, came, inv, out, inv_on):
    inv_on[...] = inv[...]
    out[...] = mine[0] + came[0]


def whole(shape):
    return pl.BlockSpec(shape, lambda i: (0,) * len(shape))


def f32(*shape):
    return jax.ShapeDtypeStruct(shape, jnp.float32)


def bf16(*shape):
    return jax.ShapeDtypeStruct(shape, jnp.bfloat16)


def call(
    kernel, out, *args, name, after=(), in_specs=None, out_specs=None, scratch=(), aliases=None
):
    def body(*refs):
        kernel(*refs[: len(args)], *refs[len(args) + len(after) :])

    return pl.pallas_call(
        body,
        grid=(1,),
        out_shape=out,
        in_specs=(in_specs or [whole(x.shape) for x in args]) + [ANY] * len(after),
        out_specs=out_specs or [whole(x.shape) for x in out],
        scratch_shapes=list(scratch),
        input_output_aliases=aliases or {},
        compiler_params=pltpu.CompilerParams(vmem_limit_bytes=LIMIT),
        cost_estimate=pl.CostEstimate(flops=1000, bytes_accessed=1000, transcendentals=0),
        name=name,
    )(*args, *after)


def make_on_device(rows, cols):
    group = rows // cols
    devices = rows * cols
    paired = cols == 4 and group == 2

    def index(plane, y, c):
        return (plane * group + y) * cols + c

    planes = [[index(p, y, p ^ d) for y in range(group) for d in range(cols)] for p in range(cols)]

    def flip(x, plane=0, y=0, col=0):
        pairs = [
            (index(p, v, c), index(p ^ plane, v ^ y, c ^ col))
            for p in range(cols) for v in range(group) for c in range(cols)
        ]
        return lax.ppermute(x, AXES, pairs)

    def on_device(trail_adjoint, panel, panel_adjoint, diag_factor, diag_inverse, diag_adjoint):
        height, size = panel.shape
        width = trail_adjoint.shape[1]
        me = lax.axis_index("row") * cols + lax.axis_index("col")

        pieces = {0: panel}
        for d in range(3, cols, 2):
            pieces[d] = flip(panel, plane=d)
        pieces[1] = flip(panel, plane=1)
        for d in range(2, cols, 2):
            pieces[d] = flip(pieces[d + 1], plane=1)

        row_blocks, order, mask = [panel], [0], cols // 2
        while mask:
            row_blocks = row_blocks + [flip(x, col=mask) for x in row_blocks]
            order = order + [o ^ mask for o in order]
            mask //= 2

        if paired:
            sets = []
            for near, far in ((1, 3), (0, 2)):
                own, other = call(
                    choose_kernel, [f32(height, size)] * 2, pieces[near], pieces[far],
                    name="choose", after=(row_blocks[1],) if near else (),
                )
                diagonal = flip(sets[0][3], plane=1) if sets else flip(other, y=1, col=2)
                sets.append([own, flip(other, col=2), flip(own, y=1), diagonal])
            chosen = own
        else:
            chosen = jnp.stack([pieces[d] for d in range(cols)] * group)

        blocks = 4
        params = [
            pltpu.with_memory_space_constraint(x, pltpu.HBM)
            for x in (panel, panel_adjoint, diag_factor, diag_inverse, diag_adjoint, trail_adjoint)
        ]
        rowt, start, base, unit, inv, trail = call(
            functools.partial(
                prepare_kernel, blocks, [order.index(d) - 1 for d in range(1, cols)]
            ),
            [bf16(2, size, cols * height), f32(size, size), f32(size, size)]
            + [bf16(2, size, size)] * 2 + [bf16(2, *trail_adjoint.shape)],
            *row_blocks[1:], *params, name="prepare", after=(chosen,),
            in_specs=[whole(panel.shape)] * (cols - 1) + [pl.BlockSpec(memory_space=pltpu.HBM)] * 6,
            out_specs=[VMEM] * 6,
            scratch=[pltpu.VMEM(trail_adjoint.shape, jnp.float32)]
            + [pltpu.VMEM((height, size), jnp.float32)] * 2
            + [pltpu.VMEM((size, size), jnp.float32)] * 3
            + [pltpu.SemaphoreType.DMA((blocks + 5,))],
        )

        if paired:
            args = sets[0] + sets[1]
            theirs = call(
                functools.partial(pick_kernel, 4), [f32(4, height, size)], *args,
                name="pick", after=(trail,),
            )[0]
            args = args + [flip(theirs, col=1)]
        else:
            args = [lax.all_to_all(chosen, AXES, 0, 0, axis_index_groups=planes, tiled=True)]
        keep, send, gram_t = call(
            functools.partial(product_kernel, group, cols, len(args)),
            [f32(cols // 2, height, size)] * 2 + [f32(size, size)],
            *args, rowt, start, trail, name="product", in_specs=[VMEM] * (len(args) + 3),
            scratch=[
                pltpu.VMEM((2, width, size), jnp.bfloat16),
                pltpu.VMEM((2, cols * height, size), jnp.bfloat16),
                pltpu.VMEM((cols * height, size), jnp.float32),
            ],
        )

        mine, theirs = call(
            add_kernel, [f32(cols // 4, height, size)] * 2,
            keep, flip(send, col=1), panel_adjoint, inv, name="add",
        )
        mask = 2
        while True:
            came = flip(theirs, col=mask)
            mask *= 2
            if mask >= cols:
                break
            mine, theirs = mine[::2] + came[::2], mine[1::2] + came[1::2]

        share = size // devices
        shares = lax.all_to_all(gram_t, AXES, 0, 0, tiled=True)
        if share % 8 == 0:
            (left_t,) = call(
                functools.partial(middle_kernel, devices, cols, share), [f32(size, size)],
                shares, base, unit, inv, name="middle", after=(theirs,),
            )
        else:
            total = jnp.sum(shares.reshape(devices, share, size), axis=0)
            inner_t = dot(
                lax.dynamic_slice_in_dim(diag_adjoint.T, me * share, share, 0)
                - dot(total, diag_inverse),
                diag_factor,
            )
            at = lax.broadcasted_iota(jnp.int32, inner_t.shape, 0) + me * share
            across = lax.broadcasted_iota(jnp.int32, inner_t.shape, 1)
            inner_t = jnp.where(across > at, inner_t, jnp.where(across == at, 0.5 * inner_t, 0.0))
            left_t = jnp.tile(dot(inner_t, diag_inverse), (devices, 1))
        gathered = lax.all_to_all(left_t, AXES, 0, 0, tiled=True)

        panel_grad, inv = call(
            panel_kernel, [f32(*panel.shape), bf16(*inv.shape)], mine, came, inv, name="panel_grad",
        )
        (diag_grad,) = call(last_kernel, [f32(size, size)], gathered, inv, name="diag_grad")
        return panel_grad, diag_grad

    return on_device


def solution(mesh):
    in_specs = (P("row", "col"), P(("row", "col"), None), P(("row", "col"), None), P(), P(), P())
    out_specs = (P(("row", "col"), None), P())
    return jax.shard_map(
        make_on_device(mesh.shape["row"], mesh.shape["col"]),
        mesh=mesh, in_specs=in_specs, out_specs=out_specs, check_vma=False,
    )
```

```python
import functools

import jax
import jax.numpy as jnp
from jax import lax
from jax.experimental import pallas as pl
from jax.experimental.pallas import tpu as pltpu
from jax.sharding import PartitionSpec as P

HIGHEST = lax.Precision.HIGHEST
AXES = ("row", "col")
ANY = pl.BlockSpec(memory_space=pl.ANY)
VMEM = pl.BlockSpec(memory_space=pltpu.VMEM)
LIMIT = 16 * 1024 * 1024


def dot(a, b, precision=HIGHEST):
    return jnp.dot(a, b, precision=precision, preferred_element_type=jnp.float32)


def dot_t(a, b, precision=HIGHEST):
    return lax.dot_general(
        a, b, (((0,), (0,)), ((), ())), precision=precision, preferred_element_type=jnp.float32
    )


def parts(x):
    high = x.astype(jnp.bfloat16)
    return high, (x - high.astype(jnp.float32)).astype(jnp.bfloat16)


def dot_parts(x, high, low):
    rows = x.shape[0]
    x = jnp.concatenate(parts(x), axis=0)
    both = dot(x, high, None) + dot(x, low, None)
    return both[:rows] + both[rows:]


def dot_three(a_high, a_low, b_high, b_low):
    return dot(a_high, b_high, None) + dot(a_high, b_low, None) + dot(a_low, b_high, None)


def needs_first():
    return (lax.axis_index("row") // 2 + lax.axis_index("col")) % 2 == 1


def choose_kernel(near, far, own, other):
    mine = lax.axis_index("col") // 2 == lax.axis_index("row") // 4

    @pl.when(mine)
    def _():
        own[...] = near[...]
        other[...] = far[...]

    @pl.when(jnp.logical_not(mine))
    def _():
        own[...] = far[...]
        other[...] = near[...]


def pick_kernel(count, *refs):
    first, second, out = refs[:count], refs[count : 2 * count], refs[-1]

    @pl.when(needs_first())
    def _():
        for i, ref in enumerate(second):
            out[i] = ref[...]

    @pl.when(jnp.logical_not(needs_first()))
    def _():
        for i, ref in enumerate(first):
            out[i] = ref[...]


def prepare_kernel(blocks, places, *refs):
    rows_of, refs = refs[: len(places)], refs[len(places) :]
    panel, adjoint, factor, inverse, corner, trail = refs[:6]
    rowt, start, base, unit, inv, trail_parts = refs[6:12]
    landing, here, sems = refs[12], refs[13:-1], refs[-1]
    rows = trail.shape[0] // blocks
    small = [
        pltpu.make_async_copy(ref, to, sems.at[blocks + i])
        for i, (ref, to) in enumerate(zip((panel, adjoint, factor, inverse, corner), here))
    ]
    large = []
    for i in range(blocks):
        at = pl.ds(i * rows, rows)
        large.append(pltpu.make_async_copy(trail.at[at], landing.at[at], sems.at[i]))
    for copy in small + large:
        copy.start()
    for copy in small:
        copy.wait()
    panel, adjoint, factor, inverse, corner = here
    height = adjoint.shape[0]
    for d, block in enumerate([panel] + [rows_of[i] for i in places]):
        high, low = parts(block[...].T)
        rowt[0, :, d * height : (d + 1) * height] = high
        rowt[1, :, d * height : (d + 1) * height] = low
    start[...] = dot_t(panel[...], adjoint[...])
    base[...] = dot_t(corner[...], factor[...])
    unit[0], unit[1] = parts(dot(inverse[...], factor[...]))
    inv[0], inv[1] = parts(inverse[...])
    for i in range(blocks):
        large[i].wait()
        at = pl.ds(i * rows, rows)
        for piece in range(trail.shape[1] // height):
            high, low = parts(landing[at, piece * height : (piece + 1) * height])
            to = slice(piece // 2 * height, (piece // 2 + 1) * height)
            trail_parts[0, piece % 2, at, to] = high
            trail_parts[1, piece % 2, at, to] = low


def fill_all(group, cols, core, pieces, wide):
    height = pieces.shape[1]
    plane = lax.axis_index("row") // group
    for y in range(group):
        for c in range(core, cols, 2):
            at = pl.ds((y * cols + c) // 2 * height, height)
            wide[0, at, :], wide[1, at, :] = parts(pieces[y * cols + (plane ^ c)])


def fill_four(pieces, wide):
    place = lax.axis_index("row") % 2 * 2 + lax.axis_index("col") // 2
    for i, piece in enumerate(pieces):
        height = piece.shape[0]
        at = pl.ds(pl.multiple_of((place ^ i) * height, height), height)
        wide[0, at, :], wide[1, at, :] = parts(piece[...])


def first_kernel(group, cols, *refs):
    pieces, (trail, out, wide) = refs[:-3], refs[-3:]
    core = 0
    if len(pieces) == 1:
        fill_all(group, cols, core, pieces[0], wide)
    else:
        core = lax.axis_index("col") % 2

        @pl.when(needs_first())
        def _():
            fill_four(pieces[:4], wide)

        @pl.when(jnp.logical_not(needs_first()))
        def _():
            fill_four(pieces[4:], wide)

    height = out.shape[0] // cols
    for i in range(cols):
        at = pl.ds(i * height, height)
        out[at, :] = dot_three(trail[0, core, at, :], trail[1, core, at, :], wide[0], wide[1])


def second_kernel(
    group, cols, paired,
    came, before, rowt, start, trail, keep, send, gram_t, wide, split, image,
):
    core = 1
    if paired:
        core = 1 - lax.axis_index("col") % 2
        fill_four([came.at[i] for i in range(4)], wide)
    else:
        fill_all(group, cols, core, came, wide)
    height = image.shape[0] // cols
    for i in range(cols):
        at = pl.ds(i * height, height)
        image[at, :] = before[at, :] + dot_three(
            trail[0, core, at, :], trail[1, core, at, :], wide[0], wide[1]
        )
    col = lax.axis_index("col")
    for d in range(cols):
        block = image[pl.ds(pl.multiple_of((d ^ col) * height, height), height), :]
        at = pl.ds(d * height, height)
        split[0, at, :], split[1, at, :] = parts(block)
        (send if d % 2 else keep)[d // 2] = block
    gram_t[...] = start[...] - 2.0 * dot_three(rowt[0], rowt[1], split[0], split[1])


def middle_kernel(devices, cols, share, shares, base, unit, inv, out):
    total = shares[pl.ds(0, share), :]
    for i in range(1, devices):
        total = total + shares[pl.ds(i * share, share), :]
    me = lax.axis_index("row") * cols + lax.axis_index("col")
    first = pl.multiple_of(me * share, share)
    inner_t = base[pl.ds(first, share), :] - dot_parts(total, unit[0], unit[1])
    at = lax.broadcasted_iota(jnp.int32, inner_t.shape, 0) + first
    across = lax.broadcasted_iota(jnp.int32, inner_t.shape, 1)
    inner_t = jnp.where(across > at, inner_t, jnp.where(across == at, 0.5 * inner_t, 0.0))
    left_t = dot_parts(inner_t, inv[0], inv[1])
    for i in range(devices):
        out[pl.ds(i * share, share), :] = left_t


def last_kernel(left_t, inv, out):
    full = dot_parts(left_t[...].T, inv[0], inv[1])
    at = lax.broadcasted_iota(jnp.int32, full.shape, 0)
    across = lax.broadcasted_iota(jnp.int32, full.shape, 1)
    out[...] = jnp.where(across < at, full, jnp.where(across == at, 0.5 * full, 0.0))


def add_kernel(keep, came, adjoint, inv, mine, theirs):
    for i in range(keep.shape[0] // 2):
        own = -2.0 * (keep[2 * i] + came[2 * i])
        mine[i] = dot_parts(own if i else adjoint[...] + own, inv[0], inv[1])
        theirs[i] = dot_parts(-2.0 * (keep[2 * i + 1] + came[2 * i + 1]), inv[0], inv[1])


def panel_kernel(mine, came, inv, out, inv_on):
    inv_on[...] = inv[...]
    out[...] = mine[0] + came[0]


def whole(shape):
    return pl.BlockSpec(shape, lambda i: (0,) * len(shape))


def f32(*shape):
    return jax.ShapeDtypeStruct(shape, jnp.float32)


def bf16(*shape):
    return jax.ShapeDtypeStruct(shape, jnp.bfloat16)


def call(
    kernel, out, *args, name, after=(), in_specs=None, out_specs=None, scratch=(), aliases=None
):
    def body(*refs):
        kernel(*refs[: len(args)], *refs[len(args) + len(after) :])

    return pl.pallas_call(
        body,
        grid=(1,),
        out_shape=out,
        in_specs=(in_specs or [whole(x.shape) for x in args]) + [ANY] * len(after),
        out_specs=out_specs or [whole(x.shape) for x in out],
        scratch_shapes=list(scratch),
        input_output_aliases=aliases or {},
        compiler_params=pltpu.CompilerParams(vmem_limit_bytes=LIMIT),
        cost_estimate=pl.CostEstimate(flops=1000, bytes_accessed=1000, transcendentals=0),
        name=name,
    )(*args, *after)


def make_on_device(rows, cols):
    group = rows // cols
    devices = rows * cols
    paired = cols == 4 and group == 2

    def index(plane, y, c):
        return (plane * group + y) * cols + c

    planes = [[index(p, y, p ^ d) for y in range(group) for d in range(cols)] for p in range(cols)]

    def flip(x, plane=0, y=0, col=0):
        pairs = [
            (index(p, v, c), index(p ^ plane, v ^ y, c ^ col))
            for p in range(cols) for v in range(group) for c in range(cols)
        ]
        return lax.ppermute(x, AXES, pairs)

    def on_device(trail_adjoint, panel, panel_adjoint, diag_factor, diag_inverse, diag_adjoint):
        height, size = panel.shape
        width = trail_adjoint.shape[1]
        me = lax.axis_index("row") * cols + lax.axis_index("col")

        pieces = {0: panel}
        for d in range(3, cols, 2):
            pieces[d] = flip(panel, plane=d)
        pieces[1] = flip(panel, plane=1)
        for d in range(2, cols, 2):
            pieces[d] = flip(pieces[d + 1], plane=1)

        row_blocks, order, mask = [panel], [0], cols // 2
        while mask:
            row_blocks = row_blocks + [flip(x, col=mask) for x in row_blocks]
            order = order + [o ^ mask for o in order]
            mask //= 2

        if paired:
            sets = []
            for near, far in ((1, 3), (0, 2)):
                own, other = call(
                    choose_kernel, [f32(height, size)] * 2, pieces[near], pieces[far],
                    name="choose", after=(row_blocks[1],) if near else (),
                )
                diagonal = flip(sets[0][3], plane=1) if sets else flip(other, y=1, col=2)
                sets.append([own, flip(other, col=2), flip(own, y=1), diagonal])
            chosen = own
        else:
            chosen = jnp.stack([pieces[d] for d in range(cols)] * group)

        blocks = 4
        params = [
            pltpu.with_memory_space_constraint(x, pltpu.HBM)
            for x in (panel, panel_adjoint, diag_factor, diag_inverse, diag_adjoint, trail_adjoint)
        ]
        rowt, start, base, unit, inv, trail = call(
            functools.partial(
                prepare_kernel, blocks, [order.index(d) - 1 for d in range(1, cols)]
            ),
            [bf16(2, size, cols * height), f32(size, size), f32(size, size)]
            + [bf16(2, size, size)] * 2 + [bf16(2, 2, cols * height, width // 2)],
            *row_blocks[1:], *params, name="prepare", after=(chosen,),
            in_specs=[whole(panel.shape)] * (cols - 1) + [pl.BlockSpec(memory_space=pltpu.HBM)] * 6,
            out_specs=[VMEM] * 6,
            scratch=[pltpu.VMEM(trail_adjoint.shape, jnp.float32)]
            + [pltpu.VMEM((height, size), jnp.float32)] * 2
            + [pltpu.VMEM((size, size), jnp.float32)] * 3
            + [pltpu.SemaphoreType.DMA((blocks + 5,))],
        )

        if paired:
            args = sets[0] + sets[1]
            theirs = call(
                functools.partial(pick_kernel, 4), [f32(4, height, size)], *args,
                name="pick", after=(trail,),
            )[0]
            came = flip(theirs, col=1)
        else:
            came = lax.all_to_all(chosen, AXES, 0, 0, axis_index_groups=planes, tiled=True)
            args = [came]
        (before,) = call(
            functools.partial(first_kernel, group, cols), [f32(cols * height, size)],
            *args, trail, name="product_first", in_specs=[VMEM] * (len(args) + 1),
            scratch=[pltpu.VMEM((2, width // 2, size), jnp.bfloat16)],
        )
        keep, send, gram_t = call(
            functools.partial(second_kernel, group, cols, paired),
            [f32(cols // 2, height, size)] * 2 + [f32(size, size)],
            came, before, rowt, start, trail, name="product_second", in_specs=[VMEM] * 5,
            scratch=[
                pltpu.VMEM((2, width // 2, size), jnp.bfloat16),
                pltpu.VMEM((2, cols * height, size), jnp.bfloat16),
                pltpu.VMEM((cols * height, size), jnp.float32),
            ],
        )

        mine, theirs = call(
            add_kernel, [f32(cols // 4, height, size)] * 2,
            keep, flip(send, col=1), panel_adjoint, inv, name="add",
        )
        mask = 2
        while True:
            came = flip(theirs, col=mask)
            mask *= 2
            if mask >= cols:
                break
            mine, theirs = mine[::2] + came[::2], mine[1::2] + came[1::2]

        share = size // devices
        shares = lax.all_to_all(gram_t, AXES, 0, 0, tiled=True)
        if share % 8 == 0:
            (left_t,) = call(
                functools.partial(middle_kernel, devices, cols, share), [f32(size, size)],
                shares, base, unit, inv, name="middle", after=(theirs,),
            )
        else:
            total = jnp.sum(shares.reshape(devices, share, size), axis=0)
            inner_t = dot(
                lax.dynamic_slice_in_dim(diag_adjoint.T, me * share, share, 0)
                - dot(total, diag_inverse),
                diag_factor,
            )
            at = lax.broadcasted_iota(jnp.int32, inner_t.shape, 0) + me * share
            across = lax.broadcasted_iota(jnp.int32, inner_t.shape, 1)
            inner_t = jnp.where(across > at, inner_t, jnp.where(across == at, 0.5 * inner_t, 0.0))
            left_t = jnp.tile(dot(inner_t, diag_inverse), (devices, 1))
        gathered = lax.all_to_all(left_t, AXES, 0, 0, tiled=True)

        panel_grad, inv = call(
            panel_kernel, [f32(*panel.shape), bf16(*inv.shape)], mine, came, inv, name="panel_grad",
        )
        (diag_grad,) = call(last_kernel, [f32(size, size)], gathered, inv, name="diag_grad")
        return panel_grad, diag_grad

    return on_device


def solution(mesh):
    in_specs = (P("row", "col"), P(("row", "col"), None), P(("row", "col"), None), P(), P(), P())
    out_specs = (P(("row", "col"), None), P())
    return jax.shard_map(
        make_on_device(mesh.shape["row"], mesh.shape["col"]),
        mesh=mesh, in_specs=in_specs, out_specs=out_specs, check_vma=False,
    )
```

```python
import functools

import jax
import jax.numpy as jnp
from jax import lax
from jax.experimental import pallas as pl
from jax.experimental.pallas import tpu as pltpu
from jax.sharding import PartitionSpec as P

HIGHEST = lax.Precision.HIGHEST
AXES = ("row", "col")
ANY = pl.BlockSpec(memory_space=pl.ANY)
VMEM = pl.BlockSpec(memory_space=pltpu.VMEM)
LIMIT = 16 * 1024 * 1024


def dot(a, b, precision=HIGHEST):
    return jnp.dot(a, b, precision=precision, preferred_element_type=jnp.float32)


def dot_t(a, b, precision=HIGHEST):
    return lax.dot_general(
        a, b, (((0,), (0,)), ((), ())), precision=precision, preferred_element_type=jnp.float32
    )


def parts(x):
    high = x.astype(jnp.bfloat16)
    return high, (x - high.astype(jnp.float32)).astype(jnp.bfloat16)


def dot_parts(x, high, low):
    rows = x.shape[0]
    x = jnp.concatenate(parts(x), axis=0)
    both = dot(x, high, None) + dot(x, low, None)
    return both[:rows] + both[rows:]


def dot_three(a_high, a_low, b_high, b_low):
    return dot(a_high, b_high, None) + dot(a_high, b_low, None) + dot(a_low, b_high, None)


def needs_first():
    return (lax.axis_index("row") // 2 + lax.axis_index("col")) % 2 == 1


def choose_kernel(near, far, own, other):
    mine = lax.axis_index("col") // 2 == lax.axis_index("row") // 4

    @pl.when(mine)
    def _():
        own[...] = near[...]
        other[...] = far[...]

    @pl.when(jnp.logical_not(mine))
    def _():
        own[...] = far[...]
        other[...] = near[...]


def pick_kernel(count, *refs):
    first, second, out = refs[:count], refs[count : 2 * count], refs[-1]

    @pl.when(needs_first())
    def _():
        for i, ref in enumerate(second):
            out[i] = ref[...]

    @pl.when(jnp.logical_not(needs_first()))
    def _():
        for i, ref in enumerate(first):
            out[i] = ref[...]


def prepare_kernel(blocks, places, *refs):
    rows_of, refs = refs[: len(places)], refs[len(places) :]
    panel, adjoint, trail, start, trail_parts, reduced, landing, panel_here, adjoint_here = refs[:9]
    rows_here, sems = refs[9:]
    rows = trail.shape[0] // blocks
    small = [
        pltpu.make_async_copy(panel, panel_here, sems.at[blocks]),
        pltpu.make_async_copy(adjoint, adjoint_here, sems.at[blocks + 1]),
    ]
    large = []
    for i in range(blocks):
        at = pl.ds(i * rows, rows)
        large.append(pltpu.make_async_copy(trail.at[at], landing.at[at], sems.at[i]))
    for copy in small + large:
        copy.start()
    for copy in small:
        copy.wait()
    height = adjoint.shape[0]
    col = lax.axis_index("col")
    for d, block in enumerate([panel_here] + [rows_of[i] for i in places]):
        rows_here[pl.ds(pl.multiple_of((d ^ col) * height, height), height), :] = block[...]
    row_high, row_low = parts(rows_here[...].T)
    start[...] = dot_t(panel_here[...], adjoint_here[...])
    for i in range(blocks):
        large[i].wait()
        at = pl.ds(i * rows, rows)
        for piece in range(trail.shape[1] // height):
            high, low = parts(landing[at, piece * height : (piece + 1) * height])
            to = slice(piece // 2 * height, (piece // 2 + 1) * height)
            trail_parts[0, piece % 2, at, to] = high
            trail_parts[1, piece % 2, at, to] = low
    for core in range(2):
        reduced[0, core], reduced[1, core] = parts(
            dot_three(row_high, row_low, trail_parts[0, core], trail_parts[1, core])
        )


def tail_kernel(factor, inverse, corner, base, unit, inv):
    base[...] = dot_t(corner[...], factor[...])
    unit[0], unit[1] = parts(dot(inverse[...], factor[...]))
    inv[0], inv[1] = parts(inverse[...])


def fill_all(group, cols, core, pieces, wide):
    height = pieces.shape[1]
    plane = lax.axis_index("row") // group
    for y in range(group):
        for c in range(core, cols, 2):
            at = pl.ds((y * cols + c) // 2 * height, height)
            wide[0, at, :], wide[1, at, :] = parts(pieces[y * cols + (plane ^ c)])


def fill_four(pieces, wide):
    place = lax.axis_index("row") % 2 * 2 + lax.axis_index("col") // 2
    for i, piece in enumerate(pieces):
        height = piece.shape[0]
        at = pl.ds(pl.multiple_of((place ^ i) * height, height), height)
        wide[0, at, :], wide[1, at, :] = parts(piece[...])


def own_core(paired):
    return lax.axis_index("col") % 2 if paired else 0


def first_kernel(group, cols, *refs):
    pieces, (start, trail, reduced, out, gram_t, wide) = refs[:-6], refs[-6:]
    paired = len(pieces) > 1
    core = own_core(paired)
    if paired:

        @pl.when(needs_first())
        def _():
            fill_four(pieces[:4], wide)

        @pl.when(jnp.logical_not(needs_first()))
        def _():
            fill_four(pieces[4:], wide)

    else:
        fill_all(group, cols, core, pieces[0], wide)
    gram_t[...] = start[...] - 2.0 * dot_three(
        reduced[0, core], reduced[1, core], wide[0], wide[1]
    )
    height = out.shape[0] // cols
    for i in range(cols):
        at = pl.ds(i * height, height)
        out[at, :] = dot_three(trail[0, core, at, :], trail[1, core, at, :], wide[0], wide[1])


def fill_rest(group, cols, paired, came, wide):
    if paired:
        fill_four([came.at[i] for i in range(4)], wide)
    else:
        fill_all(group, cols, 1, came, wide)


def gram_kernel(group, cols, paired, came, before, reduced, gram_t, wide):
    core = 1 - own_core(paired)
    fill_rest(group, cols, paired, came, wide)
    gram_t[...] = before[...] - 2.0 * dot_three(
        reduced[0, core], reduced[1, core], wide[0], wide[1]
    )


def image_kernel(group, cols, paired, came, before, trail, keep, send, wide, image):
    core = 1 - own_core(paired)
    fill_rest(group, cols, paired, came, wide)
    height = image.shape[0] // cols
    for i in range(cols):
        at = pl.ds(i * height, height)
        image[at, :] = before[at, :] + dot_three(
            trail[0, core, at, :], trail[1, core, at, :], wide[0], wide[1]
        )
    col = lax.axis_index("col")
    for d in range(cols):
        block = image[pl.ds(pl.multiple_of((d ^ col) * height, height), height), :]
        (send if d % 2 else keep)[d // 2] = block


def middle_kernel(devices, cols, share, shares, base, unit, inv, out):
    total = shares[pl.ds(0, share), :]
    for i in range(1, devices):
        total = total + shares[pl.ds(i * share, share), :]
    me = lax.axis_index("row") * cols + lax.axis_index("col")
    first = pl.multiple_of(me * share, share)
    inner_t = base[pl.ds(first, share), :] - dot_parts(total, unit[0], unit[1])
    at = lax.broadcasted_iota(jnp.int32, inner_t.shape, 0) + first
    across = lax.broadcasted_iota(jnp.int32, inner_t.shape, 1)
    inner_t = jnp.where(across > at, inner_t, jnp.where(across == at, 0.5 * inner_t, 0.0))
    left_t = dot_parts(inner_t, inv[0], inv[1])
    for i in range(devices):
        out[pl.ds(i * share, share), :] = left_t


def last_kernel(left_t, inv, out):
    full = dot_parts(left_t[...].T, inv[0], inv[1])
    at = lax.broadcasted_iota(jnp.int32, full.shape, 0)
    across = lax.broadcasted_iota(jnp.int32, full.shape, 1)
    out[...] = jnp.where(across < at, full, jnp.where(across == at, 0.5 * full, 0.0))


def add_kernel(keep, came, adjoint, inv, mine, theirs):
    for i in range(keep.shape[0] // 2):
        own = -2.0 * (keep[2 * i] + came[2 * i])
        mine[i] = dot_parts(own if i else adjoint[...] + own, inv[0], inv[1])
        theirs[i] = dot_parts(-2.0 * (keep[2 * i + 1] + came[2 * i + 1]), inv[0], inv[1])


def panel_kernel(mine, came, inv, out, inv_on):
    inv_on[...] = inv[...]
    out[...] = mine[0] + came[0]


def whole(shape):
    return pl.BlockSpec(shape, lambda i: (0,) * len(shape))


def f32(*shape):
    return jax.ShapeDtypeStruct(shape, jnp.float32)


def bf16(*shape):
    return jax.ShapeDtypeStruct(shape, jnp.bfloat16)


def call(
    kernel, out, *args, name, after=(), in_specs=None, out_specs=None, scratch=(), aliases=None
):
    def body(*refs):
        kernel(*refs[: len(args)], *refs[len(args) + len(after) :])

    return pl.pallas_call(
        body,
        grid=(1,),
        out_shape=out,
        in_specs=(in_specs or [VMEM] * len(args)) + [ANY] * len(after),
        out_specs=out_specs or [VMEM] * len(out),
        scratch_shapes=list(scratch),
        input_output_aliases=aliases or {},
        compiler_params=pltpu.CompilerParams(vmem_limit_bytes=LIMIT),
        cost_estimate=pl.CostEstimate(flops=1000, bytes_accessed=1000, transcendentals=0),
        name=name,
    )(*args, *after)


def make_on_device(rows, cols):
    group = rows // cols
    devices = rows * cols
    paired = cols == 4 and group == 2

    def index(plane, y, c):
        return (plane * group + y) * cols + c

    planes = [[index(p, y, p ^ d) for y in range(group) for d in range(cols)] for p in range(cols)]

    def flip(x, plane=0, y=0, col=0):
        pairs = [
            (index(p, v, c), index(p ^ plane, v ^ y, c ^ col))
            for p in range(cols) for v in range(group) for c in range(cols)
        ]
        return lax.ppermute(x, AXES, pairs)

    def on_device(trail_adjoint, panel, panel_adjoint, diag_factor, diag_inverse, diag_adjoint):
        height, size = panel.shape
        width = trail_adjoint.shape[1]
        me = lax.axis_index("row") * cols + lax.axis_index("col")

        pieces = {0: panel}
        for d in range(3, cols, 2):
            pieces[d] = flip(panel, plane=d)
        pieces[1] = flip(panel, plane=1)
        for d in range(2, cols, 2):
            pieces[d] = flip(pieces[d + 1], plane=1)

        row_blocks, order, mask = [panel], [0], cols // 2
        while mask:
            row_blocks = row_blocks + [flip(x, col=mask) for x in row_blocks]
            order = order + [o ^ mask for o in order]
            mask //= 2

        if paired:
            sets = []
            for near, far in ((1, 3), (0, 2)):
                own, other = call(
                    choose_kernel, [f32(height, size)] * 2, pieces[near], pieces[far],
                    name="choose", after=(row_blocks[1],) if near else (row_blocks[2], row_blocks[3]),
                )
                diagonal = flip(sets[0][3], plane=1) if sets else flip(other, y=1, col=2)
                sets.append([own, flip(other, col=2), flip(own, y=1), diagonal])
            chosen = own
        else:
            chosen = jnp.stack([pieces[d] for d in range(cols)] * group)

        blocks = 4
        params = [
            pltpu.with_memory_space_constraint(x, pltpu.HBM)
            for x in (panel, panel_adjoint, trail_adjoint)
        ]
        rows, half = cols * height, width // 2
        start, trail, reduced = call(
            functools.partial(
                prepare_kernel, blocks, [order.index(d) - 1 for d in range(1, cols)]
            ),
            [f32(size, size), bf16(2, 2, rows, half), bf16(2, 2, size, half)],
            *row_blocks[1:], *params, name="prepare", after=(chosen,),
            in_specs=[VMEM] * (cols - 1) + [pl.BlockSpec(memory_space=pltpu.HBM)] * 3,
            scratch=[pltpu.VMEM(trail_adjoint.shape, jnp.float32)]
            + [pltpu.VMEM((height, size), jnp.float32)] * 2
            + [pltpu.VMEM((rows, size), jnp.float32), pltpu.SemaphoreType.DMA((blocks + 2,))],
        )

        if paired:
            args = sets[0] + sets[1]
            theirs = call(
                functools.partial(pick_kernel, 4), [f32(4, height, size)], *args,
                name="pick", after=(trail,),
            )[0]
            came = flip(theirs, col=1)
        else:
            came = lax.all_to_all(chosen, AXES, 0, 0, axis_index_groups=planes, tiled=True)
            args = [came]
        wide = pltpu.VMEM((2, half, size), jnp.bfloat16)
        before, gram_t = call(
            functools.partial(first_kernel, group, cols), [f32(rows, size), f32(size, size)],
            *args, start, trail, reduced, name="product_first", scratch=[wide],
        )
        (gram_t,) = call(
            functools.partial(gram_kernel, group, cols, paired), [f32(size, size)],
            came, gram_t, reduced, name="gram", scratch=[wide],
        )
        keep, send = call(
            functools.partial(image_kernel, group, cols, paired),
            [f32(cols // 2, height, size)] * 2, came, before, trail, name="product_second",
            scratch=[wide, pltpu.VMEM((rows, size), jnp.float32)], after=(gram_t,),
        )
        base, unit, inv = call(
            tail_kernel, [f32(size, size)] + [bf16(2, size, size)] * 2,
            diag_factor, diag_inverse, diag_adjoint, name="tail", after=(keep,),
        )

        mine, theirs = call(
            add_kernel, [f32(cols // 4, height, size)] * 2,
            keep, flip(send, col=1), panel_adjoint, inv, name="add",
        )
        mask = 2
        while True:
            came = flip(theirs, col=mask)
            mask *= 2
            if mask >= cols:
                break
            mine, theirs = mine[::2] + came[::2], mine[1::2] + came[1::2]

        share = size // devices
        shares = lax.all_to_all(gram_t, AXES, 0, 0, tiled=True)
        if share % 8 == 0:
            (left_t,) = call(
                functools.partial(middle_kernel, devices, cols, share), [f32(size, size)],
                shares, base, unit, inv, name="middle", after=(theirs,),
            )
        else:
            total = jnp.sum(shares.reshape(devices, share, size), axis=0)
            inner_t = dot(
                lax.dynamic_slice_in_dim(diag_adjoint.T, me * share, share, 0)
                - dot(total, diag_inverse),
                diag_factor,
            )
            at = lax.broadcasted_iota(jnp.int32, inner_t.shape, 0) + me * share
            across = lax.broadcasted_iota(jnp.int32, inner_t.shape, 1)
            inner_t = jnp.where(across > at, inner_t, jnp.where(across == at, 0.5 * inner_t, 0.0))
            left_t = jnp.tile(dot(inner_t, diag_inverse), (devices, 1))
        gathered = lax.all_to_all(left_t, AXES, 0, 0, tiled=True)

        panel_grad, inv = call(
            panel_kernel, [f32(*panel.shape), bf16(*inv.shape)], mine, came, inv, name="panel_grad",
        )
        (diag_grad,) = call(last_kernel, [f32(size, size)], gathered, inv, name="diag_grad")
        return panel_grad, diag_grad

    return on_device


def solution(mesh):
    in_specs = (P("row", "col"), P(("row", "col"), None), P(("row", "col"), None), P(), P(), P())
    out_specs = (P(("row", "col"), None), P())
    return jax.shard_map(
        make_on_device(mesh.shape["row"], mesh.shape["col"]),
        mesh=mesh, in_specs=in_specs, out_specs=out_specs, check_vma=False,
    )
```

```python
import functools

import jax
import jax.numpy as jnp
from jax import lax
from jax.experimental import pallas as pl
from jax.experimental.pallas import tpu as pltpu
from jax.sharding import PartitionSpec as P

HIGHEST = lax.Precision.HIGHEST
AXES = ("row", "col")
ANY = pl.BlockSpec(memory_space=pl.ANY)
VMEM = pl.BlockSpec(memory_space=pltpu.VMEM)
LIMIT = 16 * 1024 * 1024


def dot(a, b, precision=HIGHEST):
    return jnp.dot(a, b, precision=precision, preferred_element_type=jnp.float32)


def dot_t(a, b, precision=HIGHEST):
    return lax.dot_general(
        a, b, (((0,), (0,)), ((), ())), precision=precision, preferred_element_type=jnp.float32
    )


def parts(x):
    high = x.astype(jnp.bfloat16)
    return high, (x - high.astype(jnp.float32)).astype(jnp.bfloat16)


def dot_parts(x, high, low):
    rows = x.shape[0]
    x = jnp.concatenate(parts(x), axis=0)
    both = dot(x, high, None) + dot(x, low, None)
    return both[:rows] + both[rows:]


def dot_three(a_high, a_low, b_high, b_low):
    return dot(a_high, b_high, None) + dot(a_high, b_low, None) + dot(a_low, b_high, None)


def needs_first():
    return (lax.axis_index("row") // 2 + lax.axis_index("col")) % 2 == 1


def choose_kernel(near, far, own, other):
    mine = lax.axis_index("col") // 2 == lax.axis_index("row") // 4

    @pl.when(mine)
    def _():
        own[...] = near[...]
        other[...] = far[...]

    @pl.when(jnp.logical_not(mine))
    def _():
        own[...] = far[...]
        other[...] = near[...]


def pick_kernel(count, *refs):
    first, second, out = refs[:count], refs[count : 2 * count], refs[-1]

    @pl.when(needs_first())
    def _():
        for i, ref in enumerate(second):
            out[i] = ref[...]

    @pl.when(jnp.logical_not(needs_first()))
    def _():
        for i, ref in enumerate(first):
            out[i] = ref[...]


def prepare_kernel(blocks, places, *refs):
    rows_of, refs = refs[: len(places)], refs[len(places) :]
    panel, adjoint, trail, start, trail_parts, reduced, landing, panel_here, adjoint_here = refs[:9]
    rows_here, sems = refs[9:]
    rows = trail.shape[0] // blocks
    small = [
        pltpu.make_async_copy(panel, panel_here, sems.at[blocks]),
        pltpu.make_async_copy(adjoint, adjoint_here, sems.at[blocks + 1]),
    ]
    large = []
    for i in range(blocks):
        at = pl.ds(i * rows, rows)
        large.append(pltpu.make_async_copy(trail.at[at], landing.at[at], sems.at[i]))
    for copy in small + large:
        copy.start()
    for copy in small:
        copy.wait()
    height = adjoint.shape[0]
    col = lax.axis_index("col")
    for d, block in enumerate([panel_here] + [rows_of[i] for i in places]):
        rows_here[pl.ds(pl.multiple_of((d ^ col) * height, height), height), :] = block[...]
    row_high, row_low = parts(rows_here[...].T)
    start[...] = dot_t(panel_here[...], adjoint_here[...])
    for i in range(blocks):
        large[i].wait()
        at = pl.ds(i * rows, rows)
        for piece in range(trail.shape[1] // height):
            high, low = parts(landing[at, piece * height : (piece + 1) * height])
            to = slice(piece // 2 * height, (piece // 2 + 1) * height)
            trail_parts[0, piece % 2, at, to] = high
            trail_parts[1, piece % 2, at, to] = low
    for core in range(2):
        reduced[0, core], reduced[1, core] = parts(
            dot_three(row_high, row_low, trail_parts[0, core], trail_parts[1, core])
        )


def tail_kernel(factor, inverse, corner, base, unit, inv):
    base[...] = dot_t(corner[...], factor[...])
    unit[0], unit[1] = parts(dot(inverse[...], factor[...]))
    inv[0], inv[1] = parts(inverse[...])


def fill_all(group, cols, core, pieces, wide):
    height = pieces.shape[1]
    plane = lax.axis_index("row") // group
    for y in range(group):
        for c in range(core, cols, 2):
            at = pl.ds((y * cols + c) // 2 * height, height)
            wide[0, at, :], wide[1, at, :] = parts(pieces[y * cols + (plane ^ c)])


def fill_four(pieces, wide):
    place = lax.axis_index("row") % 2 * 2 + lax.axis_index("col") // 2
    for i, piece in enumerate(pieces):
        height = piece.shape[0]
        at = pl.ds(pl.multiple_of((place ^ i) * height, height), height)
        wide[0, at, :], wide[1, at, :] = parts(piece[...])


def own_core(paired):
    return lax.axis_index("col") % 2 if paired else 0


def first_kernel(group, cols, *refs):
    pieces, (start, trail, reduced, out, gram_t, wide) = refs[:-6], refs[-6:]
    paired = len(pieces) > 1
    core = own_core(paired)
    if paired:

        @pl.when(needs_first())
        def _():
            fill_four(pieces[:4], wide)

        @pl.when(jnp.logical_not(needs_first()))
        def _():
            fill_four(pieces[4:], wide)

    else:
        fill_all(group, cols, core, pieces[0], wide)
    gram_t[...] = start[...] - 2.0 * dot_three(
        reduced[0, core], reduced[1, core], wide[0], wide[1]
    )
    height = out.shape[0] // cols
    for i in range(cols):
        at = pl.ds(i * height, height)
        out[at, :] = dot_three(trail[0, core, at, :], trail[1, core, at, :], wide[0], wide[1])


def fill_rest(group, cols, paired, came, wide):
    if paired:
        fill_four([came.at[i] for i in range(4)], wide)
    else:
        fill_all(group, cols, 1, came, wide)


def gram_kernel(group, cols, paired, came, before, reduced, gram_t, wide):
    core = 1 - own_core(paired)
    fill_rest(group, cols, paired, came, wide)
    gram_t[...] = before[...] - 2.0 * dot_three(
        reduced[0, core], reduced[1, core], wide[0], wide[1]
    )


def image_kernel(group, cols, paired, came, before, trail, keep, send, wide, image):
    core = 1 - own_core(paired)
    fill_rest(group, cols, paired, came, wide)
    height = image.shape[0] // cols
    for i in range(cols):
        at = pl.ds(i * height, height)
        image[at, :] = before[at, :] + dot_three(
            trail[0, core, at, :], trail[1, core, at, :], wide[0], wide[1]
        )
    col = lax.axis_index("col")
    for d in range(cols):
        block = image[pl.ds(pl.multiple_of((d ^ col) * height, height), height), :]
        (send if d % 2 else keep)[d // 2] = block


def middle_kernel(devices, cols, share, shares, base, unit, inv, out):
    total = shares[pl.ds(0, share), :]
    for i in range(1, devices):
        total = total + shares[pl.ds(i * share, share), :]
    me = lax.axis_index("row") * cols + lax.axis_index("col")
    first = pl.multiple_of(me * share, share)
    inner_t = base[pl.ds(first, share), :] - dot_parts(total, unit[0], unit[1])
    at = lax.broadcasted_iota(jnp.int32, inner_t.shape, 0) + first
    across = lax.broadcasted_iota(jnp.int32, inner_t.shape, 1)
    inner_t = jnp.where(across > at, inner_t, jnp.where(across == at, 0.5 * inner_t, 0.0))
    left_t = dot_parts(inner_t, inv[0], inv[1])
    for i in range(devices):
        out[pl.ds(i * share, share), :] = left_t


def last_kernel(mine, came, left_t, inv, panel_grad, diag_grad):
    panel_grad[...] = mine[0] + came[0]
    full = dot_parts(left_t[...].T, inv[0], inv[1])
    at = lax.broadcasted_iota(jnp.int32, full.shape, 0)
    across = lax.broadcasted_iota(jnp.int32, full.shape, 1)
    diag_grad[...] = jnp.where(across < at, full, jnp.where(across == at, 0.5 * full, 0.0))


def add_kernel(keep, came, adjoint, inv, mine, theirs):
    for i in range(keep.shape[0] // 2):
        own = -2.0 * (keep[2 * i] + came[2 * i])
        mine[i] = dot_parts(own if i else adjoint[...] + own, inv[0], inv[1])
        theirs[i] = dot_parts(-2.0 * (keep[2 * i + 1] + came[2 * i + 1]), inv[0], inv[1])


def whole(shape):
    return pl.BlockSpec(shape, lambda i: (0,) * len(shape))


def f32(*shape):
    return jax.ShapeDtypeStruct(shape, jnp.float32)


def bf16(*shape):
    return jax.ShapeDtypeStruct(shape, jnp.bfloat16)


def call(
    kernel, out, *args, name, after=(), in_specs=None, out_specs=None, scratch=(), aliases=None
):
    def body(*refs):
        kernel(*refs[: len(args)], *refs[len(args) + len(after) :])

    return pl.pallas_call(
        body,
        grid=(1,),
        out_shape=out,
        in_specs=(in_specs or [VMEM] * len(args)) + [ANY] * len(after),
        out_specs=out_specs or [VMEM] * len(out),
        scratch_shapes=list(scratch),
        input_output_aliases=aliases or {},
        compiler_params=pltpu.CompilerParams(vmem_limit_bytes=LIMIT),
        cost_estimate=pl.CostEstimate(flops=1000, bytes_accessed=1000, transcendentals=0),
        name=name,
    )(*args, *after)


def make_on_device(rows, cols):
    group = rows // cols
    devices = rows * cols
    paired = cols == 4 and group == 2

    def index(plane, y, c):
        return (plane * group + y) * cols + c

    planes = [[index(p, y, p ^ d) for y in range(group) for d in range(cols)] for p in range(cols)]

    def flip(x, plane=0, y=0, col=0):
        pairs = [
            (index(p, v, c), index(p ^ plane, v ^ y, c ^ col))
            for p in range(cols) for v in range(group) for c in range(cols)
        ]
        return lax.ppermute(x, AXES, pairs)

    def on_device(trail_adjoint, panel, panel_adjoint, diag_factor, diag_inverse, diag_adjoint):
        height, size = panel.shape
        width = trail_adjoint.shape[1]
        me = lax.axis_index("row") * cols + lax.axis_index("col")

        pieces = {0: panel}
        for d in range(3, cols, 2):
            pieces[d] = flip(panel, plane=d)
        pieces[1] = flip(panel, plane=1)
        for d in range(2, cols, 2):
            pieces[d] = flip(pieces[d + 1], plane=1)

        row_blocks, order, mask = [panel], [0], cols // 2
        while mask:
            row_blocks = row_blocks + [flip(x, col=mask) for x in row_blocks]
            order = order + [o ^ mask for o in order]
            mask //= 2

        if paired:
            sets = []
            for near, far in ((1, 3), (0, 2)):
                own, other = call(
                    choose_kernel, [f32(height, size)] * 2, pieces[near], pieces[far],
                    name="choose", after=(row_blocks[1],) if near else (row_blocks[2], row_blocks[3]),
                )
                diagonal = flip(sets[0][3], plane=1) if sets else flip(other, y=1, col=2)
                sets.append([own, flip(other, col=2), flip(own, y=1), diagonal])
            chosen = own
        else:
            chosen = jnp.stack([pieces[d] for d in range(cols)] * group)

        blocks = 4
        params = [
            pltpu.with_memory_space_constraint(x, pltpu.HBM)
            for x in (panel, panel_adjoint, trail_adjoint)
        ]
        rows, half = cols * height, width // 2
        start, trail, reduced = call(
            functools.partial(
                prepare_kernel, blocks, [order.index(d) - 1 for d in range(1, cols)]
            ),
            [f32(size, size), bf16(2, 2, rows, half), bf16(2, 2, size, half)],
            *row_blocks[1:], *params, name="prepare", after=(chosen,),
            in_specs=[VMEM] * (cols - 1) + [pl.BlockSpec(memory_space=pltpu.HBM)] * 3,
            scratch=[pltpu.VMEM(trail_adjoint.shape, jnp.float32)]
            + [pltpu.VMEM((height, size), jnp.float32)] * 2
            + [pltpu.VMEM((rows, size), jnp.float32), pltpu.SemaphoreType.DMA((blocks + 2,))],
        )

        if paired:
            args = sets[0] + sets[1]
            theirs = call(
                functools.partial(pick_kernel, 4), [f32(4, height, size)], *args,
                name="pick", after=(trail,),
            )[0]
            came = flip(theirs, col=1)
        else:
            came = lax.all_to_all(chosen, AXES, 0, 0, axis_index_groups=planes, tiled=True)
            args = [came]
        wide = pltpu.VMEM((2, half, size), jnp.bfloat16)
        before, gram_t = call(
            functools.partial(first_kernel, group, cols), [f32(rows, size), f32(size, size)],
            *args, start, trail, reduced, name="product_first", scratch=[wide],
        )
        (gram_t,) = call(
            functools.partial(gram_kernel, group, cols, paired), [f32(size, size)],
            came, gram_t, reduced, name="gram", scratch=[wide],
        )
        keep, send = call(
            functools.partial(image_kernel, group, cols, paired),
            [f32(cols // 2, height, size)] * 2, came, before, trail, name="product_second",
            scratch=[wide, pltpu.VMEM((rows, size), jnp.float32)], after=(gram_t,),
        )
        base, unit, inv = call(
            tail_kernel, [f32(size, size)] + [bf16(2, size, size)] * 2,
            diag_factor, diag_inverse, diag_adjoint, name="tail", after=(keep,),
        )

        mine, theirs = call(
            add_kernel, [f32(cols // 4, height, size)] * 2,
            keep, flip(send, col=1), panel_adjoint, inv, name="add",
        )
        mask = 2
        while True:
            came = flip(theirs, col=mask)
            mask *= 2
            if mask >= cols:
                break
            mine, theirs = mine[::2] + came[::2], mine[1::2] + came[1::2]

        share = size // devices
        shares = lax.all_to_all(gram_t, AXES, 0, 0, tiled=True)
        if share % 8 == 0:
            (left_t,) = call(
                functools.partial(middle_kernel, devices, cols, share), [f32(size, size)],
                shares, base, unit, inv, name="middle", after=(theirs,),
            )
        else:
            total = jnp.sum(shares.reshape(devices, share, size), axis=0)
            inner_t = dot(
                lax.dynamic_slice_in_dim(diag_adjoint.T, me * share, share, 0)
                - dot(total, diag_inverse),
                diag_factor,
            )
            at = lax.broadcasted_iota(jnp.int32, inner_t.shape, 0) + me * share
            across = lax.broadcasted_iota(jnp.int32, inner_t.shape, 1)
            inner_t = jnp.where(across > at, inner_t, jnp.where(across == at, 0.5 * inner_t, 0.0))
            left_t = jnp.tile(dot(inner_t, diag_inverse), (devices, 1))
        gathered = lax.all_to_all(left_t, AXES, 0, 0, tiled=True)

        panel_grad, diag_grad = call(
            last_kernel, [f32(*panel.shape), f32(size, size)], mine, came, gathered, inv,
            name="last",
        )
        return panel_grad, diag_grad

    return on_device


def solution(mesh):
    in_specs = (P("row", "col"), P(("row", "col"), None), P(("row", "col"), None), P(), P(), P())
    out_specs = (P(("row", "col"), None), P())
    return jax.shard_map(
        make_on_device(mesh.shape["row"], mesh.shape["col"]),
        mesh=mesh, in_specs=in_specs, out_specs=out_specs, check_vma=False,
    )
```

```python
import functools

import jax
import jax.numpy as jnp
from jax import lax
from jax.experimental import pallas as pl
from jax.experimental.pallas import tpu as pltpu
from jax.sharding import PartitionSpec as P

HIGHEST = lax.Precision.HIGHEST
AXES = ("row", "col")
ANY = pl.BlockSpec(memory_space=pl.ANY)
VMEM = pl.BlockSpec(memory_space=pltpu.VMEM)
LIMIT = 16 * 1024 * 1024


def dot(a, b, precision=HIGHEST):
    return jnp.dot(a, b, precision=precision, preferred_element_type=jnp.float32)


def dot_t(a, b, precision=HIGHEST):
    return lax.dot_general(
        a, b, (((0,), (0,)), ((), ())), precision=precision, preferred_element_type=jnp.float32
    )


def parts(x):
    high = x.astype(jnp.bfloat16)
    return high, (x - high.astype(jnp.float32)).astype(jnp.bfloat16)


def dot_parts(x, high, low):
    rows = x.shape[0]
    x = jnp.concatenate(parts(x), axis=0)
    both = dot(x, high, None) + dot(x, low, None)
    return both[:rows] + both[rows:]


def dot_three(a_high, a_low, b_high, b_low):
    return dot(a_high, b_high, None) + dot(a_high, b_low, None) + dot(a_low, b_high, None)


def needs_first():
    return (lax.axis_index("row") // 2 + lax.axis_index("col")) % 2 == 1


def choose_kernel(near, far, own, other):
    mine = lax.axis_index("col") // 2 == lax.axis_index("row") // 4

    @pl.when(mine)
    def _():
        own[...] = near[...]
        other[...] = far[...]

    @pl.when(jnp.logical_not(mine))
    def _():
        own[...] = far[...]
        other[...] = near[...]


def pick_kernel(count, *refs):
    first, second, out = refs[:count], refs[count : 2 * count], refs[-1]

    @pl.when(needs_first())
    def _():
        for i, ref in enumerate(second):
            out[i] = ref[...]

    @pl.when(jnp.logical_not(needs_first()))
    def _():
        for i, ref in enumerate(first):
            out[i] = ref[...]


def prepare_kernel(blocks, places, *refs):
    rows_of, refs = refs[: len(places)], refs[len(places) :]
    panel, adjoint, trail, start, trail_parts, reduced, landing, panel_here, adjoint_here = refs[:9]
    rows_here, totals, sems = refs[9:]
    rows = trail.shape[0] // blocks
    small = [
        pltpu.make_async_copy(panel, panel_here, sems.at[blocks]),
        pltpu.make_async_copy(adjoint, adjoint_here, sems.at[blocks + 1]),
    ]
    large = []
    for i in range(blocks):
        at = pl.ds(i * rows, rows)
        large.append(pltpu.make_async_copy(trail.at[at], landing.at[at], sems.at[i]))
    for copy in small + large:
        copy.start()
    for copy in small:
        copy.wait()
    height = adjoint.shape[0]
    col = lax.axis_index("col")
    for d, block in enumerate([panel_here] + [rows_of[i] for i in places]):
        rows_here[pl.ds(pl.multiple_of((d ^ col) * height, height), height), :] = block[...]
    row_high, row_low = parts(rows_here[...].T)
    start[...] = dot_t(panel_here[...], adjoint_here[...])
    for i in range(blocks):
        large[i].wait()
        at = pl.ds(i * rows, rows)
        for piece in range(trail.shape[1] // height):
            high, low = parts(landing[at, piece * height : (piece + 1) * height])
            to = slice(piece // 2 * height, (piece // 2 + 1) * height)
            trail_parts[0, piece % 2, at, to] = high
            trail_parts[1, piece % 2, at, to] = low
        for core in range(2):
            part = dot_three(
                row_high[:, i * rows : (i + 1) * rows], row_low[:, i * rows : (i + 1) * rows],
                trail_parts[0, core, at, :], trail_parts[1, core, at, :],
            )
            totals[core] = totals[core] + part if i else part
    for core in range(2):
        reduced[0, core], reduced[1, core] = parts(totals[core])


def tail_kernel(factor, inverse, corner, base, unit, inv):
    base[...] = dot_t(corner[...], factor[...])
    unit[0], unit[1] = parts(dot(inverse[...], factor[...]))
    inv[0], inv[1] = parts(inverse[...])


def fill_all(group, cols, core, pieces, wide):
    height = pieces.shape[1]
    plane = lax.axis_index("row") // group
    for y in range(group):
        for c in range(core, cols, 2):
            at = pl.ds((y * cols + c) // 2 * height, height)
            wide[0, at, :], wide[1, at, :] = parts(pieces[y * cols + (plane ^ c)])


def fill_four(pieces, wide):
    place = lax.axis_index("row") % 2 * 2 + lax.axis_index("col") // 2
    for i, piece in enumerate(pieces):
        height = piece.shape[0]
        at = pl.ds(pl.multiple_of((place ^ i) * height, height), height)
        wide[0, at, :], wide[1, at, :] = parts(piece[...])


def own_core(paired):
    return lax.axis_index("col") % 2 if paired else 0


def first_kernel(group, cols, *refs):
    pieces, (start, trail, reduced, out, gram_t, wide) = refs[:-6], refs[-6:]
    paired = len(pieces) > 1
    core = own_core(paired)
    if paired:

        @pl.when(needs_first())
        def _():
            fill_four(pieces[:4], wide)

        @pl.when(jnp.logical_not(needs_first()))
        def _():
            fill_four(pieces[4:], wide)

    else:
        fill_all(group, cols, core, pieces[0], wide)
    gram_t[...] = start[...] - 2.0 * dot_three(
        reduced[0, core], reduced[1, core], wide[0], wide[1]
    )
    height = out.shape[0] // cols
    for i in range(cols):
        at = pl.ds(i * height, height)
        out[at, :] = dot_three(trail[0, core, at, :], trail[1, core, at, :], wide[0], wide[1])


def fill_rest(group, cols, paired, came, wide):
    if paired:
        fill_four([came.at[i] for i in range(4)], wide)
    else:
        fill_all(group, cols, 1, came, wide)


def gram_kernel(group, cols, paired, came, before, reduced, gram_t, wide):
    core = 1 - own_core(paired)
    fill_rest(group, cols, paired, came, wide)
    gram_t[...] = before[...] - 2.0 * dot_three(
        reduced[0, core], reduced[1, core], wide[0], wide[1]
    )


def image_kernel(group, cols, paired, came, before, trail, keep, send, wide, image):
    core = 1 - own_core(paired)
    fill_rest(group, cols, paired, came, wide)
    height = image.shape[0] // cols
    for i in range(cols):
        at = pl.ds(i * height, height)
        image[at, :] = before[at, :] + dot_three(
            trail[0, core, at, :], trail[1, core, at, :], wide[0], wide[1]
        )
    col = lax.axis_index("col")
    for d in range(cols):
        block = image[pl.ds(pl.multiple_of((d ^ col) * height, height), height), :]
        (send if d % 2 else keep)[d // 2] = block


def middle_kernel(devices, cols, share, shares, base, unit, inv, out):
    total = shares[pl.ds(0, share), :]
    for i in range(1, devices):
        total = total + shares[pl.ds(i * share, share), :]
    me = lax.axis_index("row") * cols + lax.axis_index("col")
    first = pl.multiple_of(me * share, share)
    inner_t = base[pl.ds(first, share), :] - dot_parts(total, unit[0], unit[1])
    at = lax.broadcasted_iota(jnp.int32, inner_t.shape, 0) + first
    across = lax.broadcasted_iota(jnp.int32, inner_t.shape, 1)
    inner_t = jnp.where(across > at, inner_t, jnp.where(across == at, 0.5 * inner_t, 0.0))
    left_t = dot_parts(inner_t, inv[0], inv[1])
    for i in range(devices):
        out[pl.ds(i * share, share), :] = left_t


def last_kernel(mine, came, left_t, inv, panel_grad, diag_grad):
    panel_grad[...] = mine[0] + came[0]
    full = dot_parts(left_t[...].T, inv[0], inv[1])
    at = lax.broadcasted_iota(jnp.int32, full.shape, 0)
    across = lax.broadcasted_iota(jnp.int32, full.shape, 1)
    diag_grad[...] = jnp.where(across < at, full, jnp.where(across == at, 0.5 * full, 0.0))


def add_kernel(keep, came, adjoint, inv, mine, theirs):
    for i in range(keep.shape[0] // 2):
        own = -2.0 * (keep[2 * i] + came[2 * i])
        mine[i] = dot_parts(own if i else adjoint[...] + own, inv[0], inv[1])
        theirs[i] = dot_parts(-2.0 * (keep[2 * i + 1] + came[2 * i + 1]), inv[0], inv[1])


def whole(shape):
    return pl.BlockSpec(shape, lambda i: (0,) * len(shape))


def f32(*shape):
    return jax.ShapeDtypeStruct(shape, jnp.float32)


def bf16(*shape):
    return jax.ShapeDtypeStruct(shape, jnp.bfloat16)


def call(
    kernel, out, *args, name, after=(), in_specs=None, out_specs=None, scratch=(), limit=LIMIT
):
    def body(*refs):
        kernel(*refs[: len(args)], *refs[len(args) + len(after) :])

    return pl.pallas_call(
        body,
        grid=(1,),
        out_shape=out,
        in_specs=(in_specs or [VMEM] * len(args)) + [ANY] * len(after),
        out_specs=out_specs or [VMEM] * len(out),
        scratch_shapes=list(scratch),
        compiler_params=pltpu.CompilerParams(vmem_limit_bytes=limit),
        cost_estimate=pl.CostEstimate(flops=1000, bytes_accessed=1000, transcendentals=0),
        name=name,
    )(*args, *after)


def make_on_device(rows, cols):
    group = rows // cols
    devices = rows * cols
    paired = cols == 4 and group == 2

    def index(plane, y, c):
        return (plane * group + y) * cols + c

    planes = [[index(p, y, p ^ d) for y in range(group) for d in range(cols)] for p in range(cols)]

    def flip(x, plane=0, y=0, col=0):
        pairs = [
            (index(p, v, c), index(p ^ plane, v ^ y, c ^ col))
            for p in range(cols) for v in range(group) for c in range(cols)
        ]
        return lax.ppermute(x, AXES, pairs)

    def on_device(trail_adjoint, panel, panel_adjoint, diag_factor, diag_inverse, diag_adjoint):
        height, size = panel.shape
        width = trail_adjoint.shape[1]
        me = lax.axis_index("row") * cols + lax.axis_index("col")

        pieces = {0: panel}
        for d in range(3, cols, 2):
            pieces[d] = flip(panel, plane=d)
        pieces[1] = flip(panel, plane=1)
        for d in range(2, cols, 2):
            pieces[d] = flip(pieces[d + 1], plane=1)

        row_blocks, order, mask = [panel], [0], cols // 2
        while mask:
            row_blocks = row_blocks + [flip(x, col=mask) for x in row_blocks]
            order = order + [o ^ mask for o in order]
            mask //= 2

        if paired:
            sets = []
            for near, far in ((1, 3), (0, 2)):
                own, other = call(
                    choose_kernel, [f32(height, size)] * 2, pieces[near], pieces[far],
                    name="choose", after=(row_blocks[1],) if near else (row_blocks[2],),
                )
                diagonal = flip(sets[0][3], plane=1) if sets else flip(other, y=1, col=2)
                sets.append([own, flip(other, col=2), flip(own, y=1), diagonal])
            chosen = own
        else:
            chosen = jnp.stack([pieces[d] for d in range(cols)] * group)

        blocks = 3
        params = [
            pltpu.with_memory_space_constraint(x, pltpu.HBM)
            for x in (panel, panel_adjoint, trail_adjoint)
        ]
        rows, half = cols * height, width // 2
        start, trail, reduced = call(
            functools.partial(
                prepare_kernel, blocks, [order.index(d) - 1 for d in range(1, cols)]
            ),
            [f32(size, size), bf16(2, 2, rows, half), bf16(2, 2, size, half)],
            *row_blocks[1:], *params, name="prepare", after=(chosen,),
            in_specs=[VMEM] * (cols - 1) + [pl.BlockSpec(memory_space=pltpu.HBM)] * 3,
            scratch=[pltpu.VMEM(trail_adjoint.shape, jnp.float32)]
            + [pltpu.VMEM((height, size), jnp.float32)] * 2
            + [pltpu.VMEM((rows, size), jnp.float32), pltpu.VMEM((2, size, half), jnp.float32)]
            + [pltpu.SemaphoreType.DMA((blocks + 2,))],
            limit=LIMIT if paired else 2 * LIMIT,
        )

        if paired:
            args = sets[0] + sets[1]
            theirs = call(
                functools.partial(pick_kernel, 4), [f32(4, height, size)], *args,
                name="pick", after=(trail,),
            )[0]
            came = flip(theirs, col=1)
        else:
            came = lax.all_to_all(chosen, AXES, 0, 0, axis_index_groups=planes, tiled=True)
            args = [came]
        wide = pltpu.VMEM((2, half, size), jnp.bfloat16)
        before, gram_t = call(
            functools.partial(first_kernel, group, cols), [f32(rows, size), f32(size, size)],
            *args, start, trail, reduced, name="product_first", scratch=[wide],
        )
        (gram_t,) = call(
            functools.partial(gram_kernel, group, cols, paired), [f32(size, size)],
            came, gram_t, reduced, name="gram", scratch=[wide],
        )
        keep, send = call(
            functools.partial(image_kernel, group, cols, paired),
            [f32(cols // 2, height, size)] * 2, came, before, trail, name="product_second",
            scratch=[wide, pltpu.VMEM((rows, size), jnp.float32)], after=(gram_t,),
        )
        base, unit, inv = call(
            tail_kernel, [f32(size, size)] + [bf16(2, size, size)] * 2,
            diag_factor, diag_inverse, diag_adjoint, name="tail", after=(keep,),
        )

        mine, theirs = call(
            add_kernel, [f32(cols // 4, height, size)] * 2,
            keep, flip(send, col=1), panel_adjoint, inv, name="add",
        )
        mask = 2
        while True:
            came = flip(theirs, col=mask)
            mask *= 2
            if mask >= cols:
                break
            mine, theirs = mine[::2] + came[::2], mine[1::2] + came[1::2]

        share = size // devices
        shares = lax.all_to_all(gram_t, AXES, 0, 0, tiled=True)
        if share % 8 == 0:
            (left_t,) = call(
                functools.partial(middle_kernel, devices, cols, share), [f32(size, size)],
                shares, base, unit, inv, name="middle", after=(theirs,),
            )
        else:
            total = jnp.sum(shares.reshape(devices, share, size), axis=0)
            inner_t = dot(
                lax.dynamic_slice_in_dim(diag_adjoint.T, me * share, share, 0)
                - dot(total, diag_inverse),
                diag_factor,
            )
            at = lax.broadcasted_iota(jnp.int32, inner_t.shape, 0) + me * share
            across = lax.broadcasted_iota(jnp.int32, inner_t.shape, 1)
            inner_t = jnp.where(across > at, inner_t, jnp.where(across == at, 0.5 * inner_t, 0.0))
            left_t = jnp.tile(dot(inner_t, diag_inverse), (devices, 1))
        gathered = lax.all_to_all(left_t, AXES, 0, 0, tiled=True)

        panel_grad, diag_grad = call(
            last_kernel, [f32(*panel.shape), f32(size, size)], mine, came, gathered, inv,
            name="last",
        )
        return panel_grad, diag_grad

    return on_device


def solution(mesh):
    in_specs = (P("row", "col"), P(("row", "col"), None), P(("row", "col"), None), P(), P(), P())
    out_specs = (P(("row", "col"), None), P())
    return jax.shard_map(
        make_on_device(mesh.shape["row"], mesh.shape["col"]),
        mesh=mesh, in_specs=in_specs, out_specs=out_specs, check_vma=False,
    )
```
